256 devices in a mesh: slab: 64 (over x, z, core), cross: 4 (over y).
Axes of the slice: x: 4, y: 4, z: 8, core: 2. Of those that a mesh axis runs over, the one named last changes fastest.
Arguments:
- les_state: float32 [54, 512, 16, 128], P(None, 'slab', 'cross'), may hold values from -6 to 6
- cmc_state: float32 [54, 128, 8192], P(None, 'cross', 'slab'), may hold values from -6 to 6
- cmc_map: int32 [512, 16, 128], P('slab', 'cross'), may hold values from 0 to 8191, as said below
- pdf_index: int32 [512, 16, 128], P('slab', 'cross'), may hold values from 0 to 127
- pdf_table: float32 [128, 128], replicated, may hold values from 0.001 to 0.05
- diffusion: float32 [54], replicated, may hold values from 0.02 to 0.15
- chem_matrix: float32 [54, 54], replicated, may hold values from -0.875 to 0.875
- dissipation: float32 [128, 8192], P('cross', 'slab'), may hold values from 0.05 to 0.2
- reaction_rate: float32 [128, 8192], P('cross', 'slab'), may hold values from 0.05 to 0.5
- substeps: int32 [8192], P('slab'), may hold values from 1 to 4
Outputs:
- les_out: float32 [54, 512, 16, 128], P(None, 'slab', 'cross')
- cmc_out: float32 [54, 128, 8192], P(None, 'cross', 'slab')
The draws below stay inside these ranges and needn't reach their ends.
Inputs may be any that keep to these rules, and one draw needn't show every extreme that they name: `cmc_map`: an LES cell in plane x along the jet axis maps to a CMC cell whose index divided by 128 differs from x divided by 8 (both rounded down) by at most one.
All inputs are finite; a program needn't handle non-finite values.
Results may differ from the reference program's by a relative error of at most 0.0001.
Values sent between devices are 32-bit elements; how exact they have to be, the bound alone decides.
No kernel may reach another device: no remote copies, remote signals or barrier semaphores. Data moves between devices by JAX's collectives and lax.ppermute only.
A program may use at most 128 MiB of HBM per device.

```python
import math
import jax
import jax.numpy as jnp
from jax import lax

S = 54
NB = 128
NP = 128
CX = 8
CZ = 128
MC = 128
KMAX = 4
NX = 512
NY = 16
NCMC = 8192


def draw_cmc_map(key, part):
    plane = lax.broadcasted_iota(jnp.int32, (NX, NY, CZ), 0)
    base = plane // CX * MC + plane % CX * MC // CX
    jitter = jax.random.randint(key, (NX, NY, CZ), -MC, MC)
    return jnp.clip(base + jitter, 0, NCMC - 1).astype(jnp.int32)


def set_ends(values, own_key, low, top_value):
    shape = values.shape
    spot = [jax.random.randint(jax.random.fold_in(own_key, axis), (), 0, shape[axis]) for axis in range(len(shape))]
    values = values.at[tuple(spot)].set(low)
    longest = shape.index(max(shape))
    spot[longest] = (spot[longest] + 1) % shape[longest]
    return values.at[tuple(spot)].set(top_value)


def shard_levels(own_key, dims, cuts, least, largest):
    loudness, own = 1.0, jax.random.fold_in(own_key, 6)
    for position, shards_of in cuts:
        steps = jnp.exp(jax.random.uniform(jax.random.fold_in(own, position), (shards_of,), jnp.float32, least / len(cuts), largest / len(cuts)))
        loudness = loudness * jnp.repeat(steps, dims[position] // shards_of).reshape([-1 if axis == position else 1 for axis in range(len(dims))])
    return loudness


def gaussian(key, dims, scale, limit, split=(), held_as=jnp.bfloat16):
    array = jax.random.normal(key, dims, jnp.float32) * scale
    if len(split) > 0:
        array = shard_levels(key, dims, split, -0.22, 0.18) * array
    return jnp.clip(array, min=-limit, max=limit).astype(held_as)


def setup_inputs(seed: int = 0) -> dict:
    splits = jax.random.split(jax.random.key(seed), 11)
    les_state = gaussian(splits[0], (S, NX, NY, CZ), 1.0, 6.0, ((1, 64), (2, 4)), jnp.float32)
    cmc_state = gaussian(splits[1], (S, NB, NCMC), 1.0, 6.0, ((1, 4), (2, 64)), jnp.float32)
    cmc_map = draw_cmc_map(jax.random.fold_in(splits[10], 71), 0)
    pdf_index = set_ends(jax.random.randint(splits[3], (NX, NY, CZ), 0, NP), jax.random.fold_in(splits[3], 1), 0, NP - 1).astype(jnp.int32)
    pdf_table = jnp.clip(jnp.exp(jax.random.uniform(splits[4], (NP, NB), jnp.float32, math.log(0.001), math.log(0.05))), 0.001, 0.05)
    diffusion = jnp.clip(jnp.exp(jax.random.uniform(splits[5], (S,), jnp.float32, math.log(0.02), math.log(0.15))), 0.02, 0.15)
    chem_matrix = gaussian(splits[6], (S, S), S ** -0.5, 0.875, (), jnp.float32)
    dissipation = jnp.clip(0.05 + 0.15 * jax.random.uniform(splits[7], (NB, NCMC), jnp.float32) ** shard_levels(splits[7], (NB, NCMC), ((0, 4), (1, 64)), -0.2, 0.2), 0.05, 0.2)
    reaction_rate = jnp.clip(jnp.exp(math.log(0.5) - 2.3025851 * jax.random.uniform(splits[8], (NB, NCMC), jnp.float32) ** shard_levels(splits[8], (NB, NCMC), ((0, 4), (1, 64)), -0.2, 0.2)), 0.05, 0.5)
    substeps = set_ends(jax.random.randint(splits[9], (NCMC,), 1, KMAX + 1), jax.random.fold_in(splits[9], 1), 1, KMAX).astype(jnp.int32)
    return {"les_state": les_state, "cmc_state": cmc_state, "cmc_map": cmc_map, "pdf_index": pdf_index, "pdf_table": pdf_table, "diffusion": diffusion, "chem_matrix": chem_matrix, "dissipation": dissipation, "reaction_rate": reaction_rate, "substeps": substeps}


def reference(les_state, cmc_state, cmc_map, pdf_index, pdf_table, diffusion, chem_matrix, dissipation, reaction_rate, substeps):
    highest = lax.Precision.HIGHEST
    padded = jnp.pad(les_state, ((0, 0), (1, 1), (1, 1), (1, 1)))
    neighbours = padded[:, 2:, 1:-1, 1:-1] + padded[:, :-2, 1:-1, 1:-1]
    neighbours = neighbours + padded[:, 1:-1, 2:, 1:-1] + padded[:, 1:-1, :-2, 1:-1]
    neighbours = neighbours + padded[:, 1:-1, 1:-1, 2:] + padded[:, 1:-1, 1:-1, :-2]
    transported = les_state + diffusion[:, None, None, None] * (neighbours - 6.0 * les_state)
    species = transported.shape[0]
    flat = transported.reshape(species, -1)
    owner = cmc_map.reshape(-1).astype(jnp.int32)
    shape_id = pdf_index.reshape(-1).astype(jnp.int32)
    ncells = cmc_state.shape[2]
    nshape = pdf_table.shape[0]
    keys = owner * nshape + shape_id
    grouped = jax.ops.segment_sum(flat.T, keys, num_segments=ncells * nshape).reshape(ncells, nshape, species)
    counted = jax.ops.segment_sum(jnp.ones(owner.shape, jnp.float32), keys, num_segments=ncells * nshape).reshape(ncells, nshape)
    numer = jnp.einsum("mps,pb->sbm", grouped, pdf_table, precision=highest)
    denom = jnp.einsum("mp,pb->bm", counted, pdf_table, precision=highest)
    edged = jnp.pad(cmc_state, ((0, 0), (0, 0), (1, 1)))
    left_cells = edged[:, :, :-2]
    right_cells = edged[:, :, 2:]
    moved = cmc_state - 0.4 * (cmc_state - left_cells) + 0.1 * (right_cells - 2.0 * cmc_state + left_cells)
    blended = (numer + moved) / (denom[None] + 1.0)
    banded = jnp.pad(blended, ((0, 0), (1, 1), (0, 0)))
    state = blended + dissipation[None] * (banded[:, 2:] - 2.0 * blended + banded[:, :-2])
    for substep in range(KMAX):
        rate = jnp.dot(chem_matrix, state.reshape(species, -1), precision=highest).reshape(state.shape)
        active = (substep < substeps)[None, None, :]
        state = jnp.where(active, state + 0.5 * reaction_rate[None] * jnp.tanh(rate), state)
    projected = jnp.einsum("pb,sbm->spm", pdf_table, state, precision=highest).reshape(species, -1)
    conditional = jnp.take(projected, shape_id * ncells + owner, axis=1)
    weight_sum = jnp.sum(pdf_table, axis=1)
    conditional = conditional / weight_sum[shape_id][None, :]
    les_out = transported + 0.5 * (conditional.reshape(transported.shape) - transported)
    return les_out, state
```

```python
import functools
import jax
import jax.numpy as jnp
from jax import lax
from jax.experimental import pallas as pl
from jax.experimental.pallas import tpu as pltpu
from jax.sharding import PartitionSpec as P

F32 = jnp.float32
BF16 = jnp.bfloat16
SB = 14
LS = 16
ROWS = 32
LIMIT = pltpu.CompilerParams(vmem_limit_bytes=56 * 1024 * 1024)


def split(v):
    hi = v.astype(BF16)
    return hi, (v - hi.astype(F32)).astype(BF16)


def dot3(a_hi, a_lo, b):
    b_hi, b_lo = split(b)
    dot = functools.partial(jnp.dot, preferred_element_type=F32)
    return dot(a_hi, b_hi) + (dot(a_hi, b_lo) + dot(a_lo, b_hi))


def species_rows(ref, row):
    return jnp.concatenate(
        [
            ref[pl.ds(row, 8, stride=ROWS), :],
            ref[pl.ds(row + 8 * ROWS, 7, stride=ROWS), :],
            jnp.zeros((1, 128), F32),
        ],
        axis=0,
    )


def load_keys(pieces, keys_v, keys_s, sem):
    for k in range(4):
        keys_v[k * ROWS : (k + 1) * ROWS, :] = pieces[k][SB * ROWS : (SB + 1) * ROWS, :].astype(jnp.int32)
    copy = pltpu.make_async_copy(keys_v, keys_s, sem)
    copy.start()
    copy.wait()


def sums_kernel(p0, p1, p2, p3, table, low, own, high, g0, g1, g2, g3, x0, x1, x2, x3, keys_v, keys_s, sem):
    pieces = (p0, p1, p2, p3)
    groups = (g0, g1, g2, g3)
    stage = (x0, x1, x2, x3)
    load_keys(pieces, keys_v, keys_s, sem)

    def clear(i, c):
        for g in groups:
            g[pl.ds(i * 128, 128), :] = jnp.zeros((128, 128), F32)
        return c

    lax.fori_loop(0, 48, clear, 0)
    sub = lax.broadcasted_iota(jnp.int32, (LS, 128), 0)

    def block(row, c):
        for k in range(4):
            part = keys_v[pl.ds(k * ROWS + row, 1), :] & 7
            part = jnp.broadcast_to(part, (LS, 128))
            vals = species_rows(pieces[k], row)
            vals = jnp.where(sub == SB, 1.0, vals)
            wide = jnp.concatenate([jnp.where(part == g, vals, 0.0) for g in range(8)], axis=0)
            stage[k][...] = wide.T
        for z in range(128):
            where = [keys_s[k * ROWS + row, z] >> 3 for k in range(4)]
            old = [groups[k][pl.ds(where[k], 1), :] for k in range(4)]
            new = [stage[k][z : z + 1, :] for k in range(4)]
            for k in range(4):
                groups[k][pl.ds(where[k], 1), :] = old[k] + new[k]
        return c

    lax.fori_loop(0, ROWS, block, 0)
    t_hi, t_lo = split(table[...].T)
    for blk, out in enumerate((low, own, high)):
        def project(r, c):
            at = pl.ds(pl.multiple_of((blk * 16 + r) * 128, 128), 128)
            total = (g0[at, :] + g1[at, :]) + (g2[at, :] + g3[at, :])
            out[pl.ds(r, 128, stride=16), :] = dot3(t_hi, t_lo, total)
            return c

        lax.fori_loop(0, 16, project, 0, unroll=4)


def bin_sums(pieces, table):
    shape = jax.ShapeDtypeStruct((128 * 16, 128), F32)
    return pl.pallas_call(
        sums_kernel,
        out_shape=(shape, shape, shape),
        scratch_shapes=[pltpu.VMEM((6144, 128), F32)] * 4
        + [pltpu.VMEM((128, 128), F32)] * 4
        + [
            pltpu.VMEM((128, 128), jnp.int32),
            pltpu.SMEM((128, 128), jnp.int32),
            pltpu.SemaphoreType.DMA,
        ],
        compiler_params=LIMIT,
        name="bin_sums",
    )(*pieces, table)


def gather_kernel(p0, p1, p2, p3, low, own, high, table, o0, o1, o2, o3, proj, y0, y1, y2, y3, keys_v, keys_s, sem):
    pieces = (p0, p1, p2, p3)
    outs = (o0, o1, o2, o3)
    stage = (y0, y1, y2, y3)
    load_keys(pieces, keys_v, keys_s, sem)
    t = table[...]
    t_hi, t_lo = split(t)
    weight = jnp.broadcast_to(jnp.sum(t, axis=1, keepdims=True), (128, 128))
    for blk, src in enumerate((low, own, high)):
        def project(r, c):
            at = pl.ds(pl.multiple_of((blk * 16 + r) * 128, 128), 128)
            proj[at, :] = dot3(t_hi, t_lo, src[pl.ds(r, 128, stride=16), :]) / weight
            return c

        lax.fori_loop(0, 16, project, 0, unroll=4)

    def block(row, c):
        for k in range(4):
            for z in range(128):
                stage[k][z : z + 1, :] = proj[pl.ds(keys_s[k * ROWS + row, z] >> 3, 1), :]
        for k in range(4):
            part = keys_v[pl.ds(k * ROWS + row, 1), :] & 7
            part = jnp.broadcast_to(part, (LS, 128))
            wide = stage[k][...].T
            mean = jnp.where(part == 0, wide[0:LS], 0.0)
            for g in range(1, 8):
                mean = jnp.where(part == g, wide[g * LS : (g + 1) * LS], mean)
            vals = species_rows(pieces[k], row)
            res = vals + 0.5 * (mean - vals)
            outs[k][pl.ds(row, 8, stride=ROWS), :] = res[0:8]
            outs[k][pl.ds(row + 8 * ROWS, 6, stride=ROWS), :] = res[8:14]
        return c

    lax.fori_loop(0, ROWS, block, 0)


def relax(pieces, low, own, high, table):
    shape = jax.ShapeDtypeStruct((SB * ROWS, 128), F32)
    return pl.pallas_call(
        gather_kernel,
        out_shape=(shape,) * 4,
        scratch_shapes=[pltpu.VMEM((6144, 128), F32)]
        + [pltpu.VMEM((128, 128), F32)] * 4
        + [
            pltpu.VMEM((128, 128), jnp.int32),
            pltpu.SMEM((128, 128), jnp.int32),
            pltpu.SemaphoreType.DMA,
        ],
        compiler_params=LIMIT,
        name="relax",
    )(*pieces, low, own, high, table)


def swap_groups(tiles):
    lane = lax.broadcasted_iota(jnp.int32, (LS, 128), 1) // LS
    tiles = list(tiles)
    for d in (1, 2, 4):
        low = (lane & d) == 0
        for i in range(8):
            if i & d == 0:
                a, b = tiles[i], tiles[i + d]
                tiles[i] = jnp.where(low, a, pltpu.roll(b, LS * d, 1))
                tiles[i + d] = jnp.where(low, pltpu.roll(a, 128 - LS * d, 1), b)
    return tiles


def react_kernel(
    starts, q0, q1, q2, q3, moved, below, above, spread, rates, counts, matrix,
    out, h0, h1, h2, h3, numer,
):
    sums = (q0, q1, q2, q3)
    sends = (h0, h1, h2, h3)
    for k in range(4):
        for group in range(5):
            if group < 4:
                rows = sums[k][group * 128 : (group + 1) * 128, :]
            else:
                rows = jnp.concatenate([sums[k][512:544, :], jnp.zeros((96, 128), F32)], axis=0)
            turned = rows.T
            tiles = swap_groups([turned[g * LS : (g + 1) * LS] for g in range(8)])
            for b in range(8 if group < 4 else 2):
                numer[group * 8 + b, k * LS : (k + 1) * LS, :] = tiles[b]
    pad = jnp.zeros((2, 128), F32)

    def blend(b, k, rows):
        bottom = numer[b, SB : SB + 1, :] + 1.0
        tile = numer[b, k * LS : (k + 1) * LS, :]
        numer[b, k * LS : (k + 1) * LS, :] = (tile + jnp.concatenate([rows, pad], axis=0)) / bottom

    order = (1, 2, 3, 0)

    def own_bins(b, c):
        for k in order:
            at = starts[k] * 32 + b
            rows = jnp.concatenate(
                [moved[pl.ds(at, 8, stride=32), :], moved[pl.ds(at + 256, 6, stride=32), :]], axis=0
            )
            blend(b + 1, k, rows)
        return c

    for edge, ref in ((0, below), (33, above)):
        for k in order:
            blend(edge, k, ref[pl.ds(starts[k], SB), :])
    lax.fori_loop(0, 32, own_bins, 0, unroll=4)
    m_hi, m_lo = split(matrix[...])
    wide_m = jnp.concatenate([m_hi, m_lo, m_hi], axis=1)
    many = 8

    def bins(group, c):
        cells, scale = [], []
        for i in range(many):
            b = group * many + i
            mid = numer[b + 1]
            cells.append(mid + spread[pl.ds(b, 1), :] * (numer[b + 2] - 2.0 * mid + numer[b]))
            scale.append(0.5 * rates[pl.ds(b, 1), :])
        state_now = jnp.concatenate(cells, axis=1)
        scale = jnp.concatenate(scale, axis=1)
        left = jnp.concatenate([counts[...]] * many, axis=1)
        for substep in range(4):
            hi, lo = split(state_now)
            rate = jnp.dot(
                wide_m, jnp.concatenate([hi, hi, lo], axis=0), preferred_element_type=F32
            )
            step = jnp.where(substep < left, scale, 0.0)
            state_now = state_now + step * jnp.tanh(rate)
        for i in range(many):
            b = group * many + i
            cell = state_now[:, i * 128 : (i + 1) * 128]
            for k in range(4):
                at = starts[k] * 32 + b
                out[pl.ds(at, 8, stride=32), :] = cell[k * LS : k * LS + 8]
                out[pl.ds(at + 256, 6, stride=32), :] = cell[k * LS + 8 : k * LS + SB]
        for k in range(4):
            tiles = swap_groups(
                [state_now[k * LS : (k + 1) * LS, i * 128 : (i + 1) * 128] for i in range(8)]
            )
            at = pl.ds(pl.multiple_of(group * 128, 128), 128)
            sends[k][at, :] = jnp.concatenate(tiles, axis=0).T
        return c

    lax.fori_loop(0, 32 // many, bins, 0)


def react(starts, sums, moved, below, above, spread, rates, counts, matrix):
    smem = pl.BlockSpec(memory_space=pltpu.SMEM)
    vmem = pl.BlockSpec(memory_space=pltpu.VMEM)
    return pl.pallas_call(
        react_kernel,
        in_specs=[smem] + [vmem] * 11,
        out_specs=[vmem] * 5,
        out_shape=(jax.ShapeDtypeStruct((54 * 32, 128), F32),)
        + (jax.ShapeDtypeStruct((512, 128), F32),) * 4,
        scratch_shapes=[pltpu.VMEM((34, 64, 128), F32)],
        compiler_params=LIMIT,
        name="react",
    )(starts, *sums, moved, below, above, spread, rates, counts, matrix)


def from_behind(array, axis, by, wrap=False):
    count = lax.axis_size(axis)
    pairs = [(i, (i + by) % count) for i in range(count) if wrap or 0 <= i + by < count]
    return lax.ppermute(array, axis, pairs)


def on_device(
    les_state, cmc_state, cmc_map, pdf_index, pdf_table, diffusion, chem_matrix,
    dissipation, reaction_rate, substeps,
):
    highest = lax.Precision.HIGHEST
    j = lax.axis_index("cross")
    i = lax.axis_index("slab")
    peer = [lax.rem(j + k, 4) for k in range(4)]
    source = [lax.rem(j + 4 - k, 4) for k in range(4)]

    def start(block):
        return jnp.minimum(block * SB, 54 - SB)

    x_low = from_behind(les_state[:, 7:8], "slab", 1)
    x_high = from_behind(les_state[:, :1], "slab", -1)
    y_low = from_behind(les_state[:, :, 3:], "cross", 1)
    y_high = from_behind(les_state[:, :, :1], "cross", -1)
    m_low = from_behind(cmc_state[:, :, 127:], "slab", 1)
    m_high = from_behind(cmc_state[:, :, :1], "slab", -1)
    cat = jnp.concatenate
    near = cat([x_low, les_state[:, :-1]], 1) + cat([les_state[:, 1:], x_high], 1)
    near = near + cat([y_low, les_state[:, :, :-1]], 2) + cat([les_state[:, :, 1:], y_high], 2)
    z_pad = jnp.pad(les_state, ((0, 0), (0, 0), (0, 0), (1, 1)))
    near = near + z_pad[..., 2:] + z_pad[..., :-2]
    transported = les_state + diffusion[:, None, None, None] * (near - 6.0 * les_state)
    transported = transported.reshape(54, ROWS, 128)

    offset = cmc_map - (i - 1) * 128
    row = ((offset >> 7) * 16 + (offset & 15)) * 128 + pdf_index
    key = (row * 8 + ((offset >> 4) & 7)).astype(F32).reshape(1, ROWS, 128)
    pieces = [
        cat([lax.dynamic_slice_in_dim(transported, start(peer[k]), SB, 0), key], 0).reshape(-1, 128)
        for k in range(4)
    ]
    pieces = [pieces[0]] + [from_behind(pieces[k], "cross", k, True) for k in (1, 2, 3)]

    moved = (
        cmc_state
        - 0.4 * (cmc_state - cat([m_low, cmc_state[:, :, :-1]], 2))
        + 0.1 * (cat([cmc_state[:, :, 1:], m_high], 2) - 2.0 * cmc_state + cat([m_low, cmc_state[:, :, :-1]], 2))
    )
    b_low = from_behind(moved[:, 31:], "cross", 1).reshape(54, 128)
    b_high = from_behind(moved[:, :1], "cross", -1).reshape(54, 128)

    low, own, high = bin_sums(pieces, pdf_table)
    own = own + from_behind(low, "slab", -1) + from_behind(high, "slab", 1)
    own = jnp.pad(own, ((16, 16), (0, 0)))
    sums = [lax.dynamic_slice_in_dim(own, peer[k] * 512, 544, 0) for k in range(4)]
    sums = [sums[0]] + [from_behind(sums[k], "cross", k, True) for k in (1, 2, 3)]

    starts = jnp.stack([start(source[k]) for k in range(4)]).astype(jnp.int32)
    lane = jnp.arange(64, dtype=jnp.int32)
    held = jnp.take(starts, lane // LS)
    valid = lane % LS < SB
    pick = ((held + lane % LS)[:, None] == jnp.arange(54)[None, :]) & valid[:, None]
    again = (held == 54 - SB) & (lane % LS < 4 * SB - 54)
    once = pick & ~again[:, None]
    matrix = jnp.dot(pick.astype(F32), chem_matrix, precision=highest)
    matrix = jnp.einsum("ab,cb->ac", matrix, once.astype(F32), precision=highest)
    cmc_out, *sends = react(
        starts, sums, moved.reshape(54 * 32, 128), b_low, b_high,
        dissipation, reaction_rate, substeps.reshape(1, 128), matrix,
    )
    bins = cat([sends[0]] + [from_behind(sends[k], "cross", -k, True) for k in (1, 2, 3)], 0)
    low = from_behind(bins, "slab", 1)
    high = from_behind(bins, "slab", -1)
    table = lax.dynamic_slice_in_dim(cat([pdf_table, pdf_table], 1), j * 32, 128, 1)
    done = relax(pieces, low, bins, high, table)
    done = [done[0]] + [from_behind(done[k], "cross", -k, True) for k in (1, 2, 3)]
    les_out = jnp.zeros((54 * ROWS, 128), F32)
    for k in range(4):
        les_out = lax.dynamic_update_slice_in_dim(les_out, done[k], start(peer[k]) * ROWS, 0)
    return les_out.reshape(les_state.shape), cmc_out.reshape(cmc_state.shape)


def solution(mesh):
    return jax.shard_map(
        on_device,
        mesh=mesh,
        in_specs=(
            P(None, "slab", "cross", None),
            P(None, "cross", "slab"),
            P("slab", "cross", None),
            P("slab", "cross", None),
            P(),
            P(),
            P(),
            P("cross", "slab"),
            P("cross", "slab"),
            P("slab"),
        ),
        out_specs=(P(None, "slab", "cross", None), P(None, "cross", "slab")),
        check_vma=False,
    )
```

```python
import functools
import jax
import jax.numpy as jnp
from jax import lax
from jax.experimental import pallas as pl
from jax.experimental.pallas import tpu as pltpu
from jax.sharding import PartitionSpec as P

F32 = jnp.float32
BF16 = jnp.bfloat16
S = 54
SB = 14
LS = 16
ROWS = 32
EDGE = 216
LIMIT = pltpu.CompilerParams(vmem_limit_bytes=56 * 1024 * 1024)
SMEM = pl.BlockSpec(memory_space=pltpu.SMEM)
VMEM = pl.BlockSpec(memory_space=pltpu.VMEM)
HALF = 18 * 16


def call(kernel, name, outs, ins, scratch=(), smem=0, us=3):
    return pl.pallas_call(
        kernel,
        in_specs=[SMEM] * smem + [VMEM] * (len(ins) - smem),
        out_specs=[VMEM] * len(outs),
        out_shape=[jax.ShapeDtypeStruct((rows, 128), F32) for rows in outs],
        scratch_shapes=list(scratch),
        compiler_params=LIMIT,
        cost_estimate=pl.CostEstimate(flops=us * 10**9, bytes_accessed=us * 10**6, transcendentals=0),
        name=name,
    )(*ins)


def split(v):
    hi = v.astype(BF16)
    return hi, (v - hi.astype(F32)).astype(BF16)


def stacked(table):
    hi, lo = split(table)
    return jnp.concatenate([hi, lo, hi], axis=1)


def product(table, v):
    hi, lo = split(v)
    return jnp.dot(table, jnp.concatenate([hi, hi, lo], axis=0), preferred_element_type=F32)


def chunk_starts():
    return [128 * q for q in range(13)] + [S * ROWS - 128]


def edges_kernel(les, cmc, up, down, y_up, y_down):
    for s in range(S):
        up[s * 4 : s * 4 + 4, :] = les[s * ROWS + 28 : s * ROWS + 32, :]
        down[s * 4 : s * 4 + 4, :] = les[s * ROWS : s * ROWS + 4, :]
    y_up[...] = les[pl.ds(3, S * 8, stride=4), :]
    y_down[...] = les[pl.ds(0, S * 8, stride=4), :]
    for q, row in enumerate(chunk_starts()):
        turned = cmc[row : row + 128, :].T
        up[EDGE + q : EDGE + q + 1, :] = turned[127:128]
        down[EDGE + q : EDGE + q + 1, :] = turned[0:1]
    up[EDGE + 14 :, :] = jnp.zeros((2, 128), F32)
    down[EDGE + 14 :, :] = jnp.zeros((2, 128), F32)


def transport_kernel(info, diffusion, les, low, high, y_low, y_high, cells, shapes, p0, p1, p2, p3, side, moved):
    i, j = info[4], info[5]
    side[pl.ds(0, S * 8, stride=4), :] = jnp.where(j > 0, y_low[...], 0.0)
    side[pl.ds(3, S * 8, stride=4), :] = jnp.where(j < 3, y_high[...], 0.0)
    sub = lax.broadcasted_iota(jnp.int32, (ROWS, 128), 0) % 4
    lane = lax.broadcasted_iota(jnp.int32, (ROWS, 128), 1)
    has_low, has_high = i > 0, i < info[6] - 1
    for s in range(S):
        v = les[s * ROWS : (s + 1) * ROWS, :]
        e = side[s * ROWS : (s + 1) * ROWS, :]
        x_low = jnp.where(has_low, low[s * 4 : s * 4 + 4, :], 0.0)
        x_high = jnp.where(has_high, high[s * 4 : s * 4 + 4, :], 0.0)
        near = jnp.concatenate([v[4:], x_high], axis=0) + jnp.concatenate([x_low, v[:-4]], axis=0)
        near = near + jnp.where(sub == 3, e, pltpu.roll(v, ROWS - 1, 0))
        near = near + jnp.where(sub == 0, e, pltpu.roll(v, 1, 0))
        near = near + jnp.where(lane == 127, 0.0, pltpu.roll(v, 127, 1))
        near = near + jnp.where(lane == 0, 0.0, pltpu.roll(v, 1, 1))
        moved[s * ROWS : (s + 1) * ROWS, :] = v + diffusion[s] * (near - 6.0 * v)
    offset = cells[...] - (i - 1) * 128
    row = ((offset >> 7) * 16 + (offset & 15)) * 128 + shapes[...]
    key = (row * 8 + ((offset >> 4) & 7)).astype(F32)
    for k, piece in enumerate((p0, p1, p2, p3)):
        piece[: SB * ROWS, :] = moved[pl.ds(pl.multiple_of(info[k] * ROWS, ROWS), SB * ROWS), :]
        piece[SB * ROWS :, :] = key


def advect_kernel(info, cmc, low, high, out, b_up, b_down):
    i = info[4]
    lane = lax.broadcasted_iota(jnp.int32, (128, 128), 1)
    for q, row in enumerate(chunk_starts()):
        v = cmc[row : row + 128, :]
        first = jnp.where(i > 0, low[EDGE + q : EDGE + q + 1, :], 0.0)
        last = jnp.where(i < info[6] - 1, high[EDGE + q : EDGE + q + 1, :], 0.0)
        left = jnp.where(lane == 0, jnp.broadcast_to(first, (128, 128)).T, pltpu.roll(v, 1, 1))
        right = jnp.where(lane == 127, jnp.broadcast_to(last, (128, 128)).T, pltpu.roll(v, 127, 1))
        out[row : row + 128, :] = v - 0.4 * (v - left) + 0.1 * (right - 2.0 * v + left)
    b_up[...] = out[pl.ds(31, S, stride=32), :]
    b_down[...] = out[pl.ds(0, S, stride=32), :]


def species_rows(ref, row):
    return jnp.concatenate(
        [
            ref[pl.ds(row, 8, stride=ROWS), :],
            ref[pl.ds(row + 8 * ROWS, 7, stride=ROWS), :],
            jnp.zeros((1, 128), F32),
        ],
        axis=0,
    )


def load_keys(pieces, keys_v, rows_v, rows_s, sem):
    for k, piece in enumerate(pieces):
        key = piece[SB * ROWS : (SB + 1) * ROWS, :].astype(jnp.int32)
        keys_v[k * ROWS : (k + 1) * ROWS, :] = key & 7
        rows_v[k * ROWS : (k + 1) * ROWS, :] = key >> 3
    copy = pltpu.make_async_copy(rows_v, rows_s, sem)
    copy.start()
    return copy


def key_scratch(count):
    return [
        pltpu.VMEM((count * ROWS, 128), jnp.int32),
        pltpu.VMEM((count * ROWS, 128), jnp.int32),
        pltpu.SMEM((count * ROWS, 128), jnp.int32),
        pltpu.SemaphoreType.DMA,
    ]


def clear(groups):
    def body(n, c):
        for g in groups:
            g[pl.ds(pl.multiple_of(n * 128, 128), 128), :] = jnp.zeros((128, 128), F32)
        return c

    lax.fori_loop(0, 48, body, 0)


def scatter(lists, groups, stage, keys_v, rows_s, count):
    sub = lax.broadcasted_iota(jnp.int32, (LS, 128), 0)
    many = len(lists)
    first, second = stage[:many], stage[many:]

    def spread(n, into):
        for a, (piece, row, at) in enumerate(lists):
            part = jnp.broadcast_to(keys_v[pl.ds(at + n, 1), :], (LS, 128))
            vals = jnp.where(sub == SB, 1.0, species_rows(piece, row + n))
            wide = jnp.concatenate([jnp.where(part == g, vals, 0.0) for g in range(8)], axis=0)
            into[a][...] = wide.T

    def add(n, held):
        for z in range(128):
            where = [rows_s[at + n, z] for _, _, at in lists]
            old = [groups[a][pl.ds(where[a], 1), :] for a in range(many)]
            new = [held[a][z : z + 1, :] for a in range(many)]
            for a in range(many):
                groups[a][pl.ds(where[a], 1), :] = old[a] + new[a]

    def block(n, c):
        spread(2 * n + 1, second)
        add(2 * n, first)
        spread(jnp.minimum(2 * n + 2, count - 1), first)
        add(2 * n + 1, second)
        return c

    spread(0, first)
    lax.fori_loop(0, count // 2, block, 0)


def own_sums_kernel(piece, out, *refs):
    g, stage = refs[:3], refs[3:11]
    keys_v, rows_v, rows_s, sem = refs[11:]
    copy = load_keys((piece,), keys_v, rows_v, rows_s, sem)
    groups = (out, *g)
    clear(groups)
    copy.wait()
    scatter([(piece, 8 * a, 8 * a) for a in range(4)], groups, stage, keys_v, rows_s, 8)

    def total(n, c):
        at = pl.ds(pl.multiple_of(n * 128, 128), 128)
        out[at, :] = (out[at, :] + g[0][at, :]) + (g[1][at, :] + g[2][at, :])
        return c

    lax.fori_loop(0, 48, total, 0)


def own_sums(piece):
    scratch = [pltpu.VMEM((6144, 128), F32)] * 3 + [pltpu.VMEM((128, 128), F32)] * 8 + key_scratch(1)
    return call(own_sums_kernel, "own_sums", [6144], [piece], scratch, us=10)[0]


def bin_sums_kernel(*refs):
    p = refs[0:3]
    g0, bins = refs[3:5]
    outs = refs[5:11]
    g = refs[11:17]
    stage = refs[17:29]
    keys_v, rows_v, rows_s, sem = refs[29:]
    copy = load_keys(p, keys_v, rows_v, rows_s, sem)
    clear(g)
    copy.wait()
    lists = [(p[a], h * 16, ROWS * a + h * 16) for a in range(3) for h in range(2)]
    scatter(lists, g, stage, keys_v, rows_s, 16)
    wide = stacked(bins[...])
    for blk in range(3):
        def project(n, c):
            total = []
            for r in (2 * n, 2 * n + 1):
                at = pl.ds(pl.multiple_of((blk * 16 + r) * 128, 128), 128)
                total.append(
                    ((g0[at, :] + g[0][at, :]) + (g[1][at, :] + g[2][at, :]))
                    + ((g[3][at, :] + g[4][at, :]) + g[5][at, :])
                )
            res = product(wide, jnp.concatenate(total, axis=1))
            for i in range(2):
                for h in range(2):
                    for k in range(4):
                        cut = k * 40 + h * 16
                        at = pl.ds(k * HALF + 2 * n + i, 18, stride=16)
                        outs[blk * 2 + h][at, :] = res[cut : cut + 18, i * 128 : (i + 1) * 128]
            return c

        lax.fori_loop(0, 8, project, 0, unroll=2)


def bin_sums(pieces, own, bins):
    scratch = [pltpu.VMEM((6144, 128), F32)] * 6 + [pltpu.VMEM((128, 128), F32)] * 12 + key_scratch(3)
    out = call(bin_sums_kernel, "bin_sums", [4 * HALF] * 6, [*pieces, own, bins], scratch, us=25)
    return out[0:2], out[2:4], out[4:6]


def gather(piece, out, proj, stage, keys_v, rows_s, at):
    first, second = stage[:2], stage[2:]

    def fetch(n, into):
        for a in range(2):
            for z in range(128):
                into[a][z : z + 1, :] = proj[pl.ds(rows_s[at + n * 2 + a, z], 1), :]

    def finish(n, held):
        for a in range(2):
            row = n * 2 + a
            part = jnp.broadcast_to(keys_v[pl.ds(at + row, 1), :], (LS, 128))
            wide = held[a][...].T
            mean = jnp.where(part == 0, wide[0:LS], 0.0)
            for g in range(1, 8):
                mean = jnp.where(part == g, wide[g * LS : (g + 1) * LS], mean)
            vals = species_rows(piece, row)
            res = vals + 0.5 * (mean - vals)
            out[pl.ds(row, 8, stride=ROWS), :] = res[0:8]
            out[pl.ds(row + 8 * ROWS, 6, stride=ROWS), :] = res[8:14]

    def block(n, c):
        fetch(2 * n + 1, second)
        finish(2 * n, first)
        fetch(jnp.minimum(2 * n + 2, ROWS // 2 - 1), first)
        finish(2 * n + 1, second)
        return c

    fetch(0, first)
    lax.fori_loop(0, ROWS // 4, block, 0)


def far_kernel(*refs):
    info, piece = refs[0:2]
    blocks = refs[2:8]
    table, out, proj = refs[8:11]
    stage = refs[11:15]
    keys_v, rows_v, rows_s, sem = refs[15:]
    copy = load_keys((piece,), keys_v, rows_v, rows_s, sem)
    t = table[...]
    wide = stacked(t)
    weight = jnp.broadcast_to(jnp.sum(t, axis=1, keepdims=True), (128, 128))
    held = [((b + 4 - info[5]) & 3) * 256 for b in range(4)]
    for blk in range(3):
        def project(n, c):
            src = []
            for r in (2 * n, 2 * n + 1):
                rows = [
                    blocks[blk * 2 + h][pl.ds(held[b] + r, 16, stride=16), :]
                    for b in range(4) for h in range(2)
                ]
                src.append(jnp.concatenate(rows, axis=0))
            res = product(wide, jnp.concatenate(src, axis=1))
            for i in range(2):
                at = pl.ds(pl.multiple_of((blk * 16 + 2 * n + i) * 128, 128), 128)
                proj[at, :] = res[:, i * 128 : (i + 1) * 128] / weight
            return c

        lax.fori_loop(0, 8, project, 0, unroll=2)
    copy.wait()
    gather(piece, out, proj, stage, keys_v, rows_s, 0)


def near_kernel(*refs):
    count = (len(refs) - 9) // 2
    pieces, proj, outs = refs[:count], refs[count], refs[count + 1 : 2 * count + 1]
    stage = refs[2 * count + 1 : 2 * count + 5]
    keys_v, rows_v, rows_s, sem = refs[2 * count + 5 :]
    load_keys(pieces, keys_v, rows_v, rows_s, sem).wait()
    for a in range(count):
        gather(pieces[a], outs[a], proj, stage, keys_v, rows_s, a * ROWS)


def assemble_kernel(info, *refs):
    for k in range(4):
        at = pl.ds(pl.multiple_of(info[k] * ROWS, ROWS), SB * ROWS)
        refs[4][at, :] = refs[k][...]


def relax_far(info, piece, blocks, table):
    scratch = [pltpu.VMEM((128, 128), F32)] * 4 + key_scratch(1)
    return call(far_kernel, "relax_far", [SB * ROWS, 6144], [info, piece, *blocks, table], scratch, smem=1, us=12)


def relax_near(pieces, proj, name):
    scratch = [pltpu.VMEM((128, 128), F32)] * 4 + key_scratch(len(pieces))
    return call(near_kernel, name, [SB * ROWS] * len(pieces), [*pieces, proj], scratch, us=7 * len(pieces))


def swap_groups(tiles):
    lane = lax.broadcasted_iota(jnp.int32, (LS, 128), 1) // LS
    tiles = list(tiles)
    for d in (1, 2, 4):
        low = (lane & d) == 0
        for i in range(8):
            if i & d == 0:
                a, b = tiles[i], tiles[i + d]
                tiles[i] = jnp.where(low, a, pltpu.roll(b, LS * d, 1))
                tiles[i + d] = jnp.where(low, pltpu.roll(a, 128 - LS * d, 1), b)
    return tiles


def react_kernel(
    half, starts, info, q0, q1, q2, q3, moved, spread, rates, counts, matrix,
    out, h0, h1, h2, h3, numer,
):
    sums = (q0, q1, q2, q3)
    sends = (h0, h1, h2, h3)
    for k in range(4):
        for group in range(3):
            if group < 2:
                rows = sums[k][group * 128 : (group + 1) * 128, :]
            else:
                rows = jnp.concatenate([sums[k][256:HALF, :], jnp.zeros((96, 128), F32)], axis=0)
            turned = rows.T
            tiles = swap_groups([turned[g * LS : (g + 1) * LS] for g in range(8)])
            for b in range(8 if group < 2 else 2):
                numer[group * 8 + b, k * LS : (k + 1) * LS, :] = tiles[b]
    pad = jnp.zeros((2, 128), F32)

    def blend(n, k, rows):
        bottom = numer[n, SB : SB + 1, :] + 1.0
        tile = numer[n, k * LS : (k + 1) * LS, :]
        numer[n, k * LS : (k + 1) * LS, :] = (tile + jnp.concatenate([rows, pad], axis=0)) / bottom

    order = (1, 2, 3, 0)

    def own_bins(n, c):
        for k in order:
            at = starts[k] * 32 + n + (16 * half - 1)
            rows = jnp.concatenate(
                [moved[pl.ds(at, 8, stride=32), :], moved[pl.ds(at + 256, 6, stride=32), :]], axis=0
            )
            blend(n, k, rows)
        return c

    edge, ref, there = ((0, q1, info[5] > 0), (17, q3, info[5] < 3))[half]
    for k in order:
        blend(edge, k, jnp.where(there, ref[pl.ds(HALF + starts[k], SB), :], 0.0))
    lax.fori_loop(1 - half, 18 - half, own_bins, 0, unroll=True)
    m_hi, m_lo = split(matrix[...])
    wide_m = jnp.concatenate([m_hi, m_lo, m_hi], axis=1)
    many = 8

    def bins(group, c):
        cells, scale = [], []
        for i in range(many):
            n = group * many + i
            b = 16 * half + n
            mid = numer[n + 1]
            cells.append(mid + spread[pl.ds(b, 1), :] * (numer[n + 2] - 2.0 * mid + numer[n]))
            scale.append(0.5 * rates[pl.ds(b, 1), :])
        state_now = jnp.concatenate(cells, axis=1)
        scale = jnp.concatenate(scale, axis=1)
        left = jnp.concatenate([counts[...]] * many, axis=1)
        for substep in range(4):
            hi, lo = split(state_now)
            rate = jnp.dot(
                wide_m, jnp.concatenate([hi, hi, lo], axis=0), preferred_element_type=F32
            )
            step = jnp.where(substep < left, scale, 0.0)
            state_now = state_now + step * jnp.tanh(rate)
        for k in range(4):
            tiles = swap_groups(
                [state_now[k * LS : (k + 1) * LS, i * 128 : (i + 1) * 128] for i in range(8)]
            )
            at = pl.ds(pl.multiple_of(group * 128, 128), 128)
            sends[k][at, :] = jnp.concatenate(tiles, axis=0).T
        for i in range(many):
            n = group * many + i
            cell = state_now[:, i * 128 : (i + 1) * 128]
            for k in range(4):
                at = starts[k] * 16 + n
                out[pl.ds(at, 8, stride=16), :] = cell[k * LS : k * LS + 8]
                out[pl.ds(at + 128, 6, stride=16), :] = cell[k * LS + 8 : k * LS + SB]
        return c

    lax.fori_loop(0, 16 // many, bins, 0, unroll=True)


def react(half, starts, info, sums, moved, spread, rates, counts, matrix):
    return call(
        functools.partial(react_kernel, half), "react_upper" if half else "react_lower",
        [S * 16] + [256] * 4,
        [starts, info, *sums, moved, spread, rates, counts, matrix],
        [pltpu.VMEM((18, 64, 128), F32)], smem=2, us=6,
    )


def shift(array, axis, by):
    count = lax.axis_size(axis)
    return lax.ppermute(array, axis, [(n, (n + by) % count) for n in range(count)])


def on_device(
    les_state, cmc_state, cmc_map, pdf_index, pdf_table, diffusion, chem_matrix,
    dissipation, reaction_rate, substeps,
):
    highest = lax.Precision.HIGHEST
    i, j = lax.axis_index("slab"), lax.axis_index("cross")
    peer = [lax.rem(j + k, 4) for k in range(4)]
    source = [lax.rem(j + 4 - k, 4) for k in range(4)]

    def start(block):
        return jnp.minimum(block * SB, S - SB)

    info = jnp.stack([start(p) for p in peer] + [i, j, jnp.int32(lax.axis_size("slab"))]).astype(jnp.int32)
    starts = jnp.stack([start(p) for p in source]).astype(jnp.int32)
    les = les_state.reshape(S * ROWS, 128)
    cmc = cmc_state.reshape(S * 32, 128)
    up, down, y_up, y_down = call(edges_kernel, "edges", [EDGE + 16] * 2 + [S * 8] * 2, [les, cmc])
    low, high = shift(up, "slab", 1), shift(down, "slab", -1)
    y_low, y_high = shift(y_up, "cross", 1), shift(y_down, "cross", -1)
    pieces = call(
        transport_kernel, "transport", [(SB + 1) * ROWS] * 4,
        [info, diffusion, les, low, high, y_low, y_high, cmc_map.reshape(ROWS, 128), pdf_index.reshape(ROWS, 128)],
        [pltpu.VMEM((S * ROWS, 128), F32)] * 2, smem=2,
    )
    pieces = [pieces[0]] + [shift(pieces[k], "cross", k) for k in (1, 2, 3)]
    turned = jnp.pad(pdf_table.T, ((1, 7), (0, 0)))
    bins = jnp.concatenate([lax.dynamic_slice_in_dim(turned, p * 32, 40, 0) for p in peer], 0)
    lane = jnp.arange(64, dtype=jnp.int32)
    held = start(lax.rem(j + 4 - lane // LS, 4))
    pick = ((held + lane % LS)[:, None] == jnp.arange(S)[None, :]) & (lane % LS < SB)[:, None]
    again = (held == S - SB) & (lane % LS < 4 * SB - S)
    once = pick & ~again[:, None]
    matrix = jnp.dot(pick.astype(F32), chem_matrix, precision=highest)
    matrix = jnp.einsum("ab,cb->ac", matrix, once.astype(F32), precision=highest)

    own = own_sums(pieces[0])
    below, here, above = bin_sums(pieces[1:], own, bins)
    got = [(shift(below[h], "slab", -1), shift(above[h], "slab", 1)) for h in range(2)]
    cmc, here = lax.optimization_barrier((cmc, here))
    moved, b_up, b_down = call(advect_kernel, "advect", [S * 32, S, S], [info, cmc, low, high], smem=1)
    here, moved = lax.optimization_barrier((here, moved))
    cat = jnp.concatenate
    sums = []
    for h in range(2):
        total = here[h] + got[h][0] + got[h][1]
        part = [total[k * HALF : (k + 1) * HALF] for k in range(4)]
        if h:
            part[3] = cat([part[3], b_down], 0)
        else:
            part[1] = cat([part[1], b_up], 0)
        sums.append([part[0]] + [shift(part[k], "cross", k) for k in (1, 2, 3)])
    halves, sends = [], []
    for h in range(2):
        if h:
            sums[1], halves[0] = lax.optimization_barrier((sums[1], halves[0]))
        state, *parts = react(
            h, starts, info, sums[h], moved, dissipation, reaction_rate, substeps.reshape(1, 128), matrix
        )
        halves.append(state)
        sends.append(parts)
    low, high, here = [], [], []
    for h in range(2):
        if h:
            sends[1], got = lax.optimization_barrier((sends[1], got))
        got = [sends[h][0]] + [shift(sends[h][k], "cross", -k) for k in (1, 2, 3)]
        here.append(got)
    for h in range(2):
        here[h] = cat(lax.optimization_barrier(here[h]), 0)
        low.append(shift(here[h], "slab", 1))
        high.append(shift(here[h], "slab", -1))
    cmc_out = cat([half.reshape(S, 16, 128) for half in halves], 1)
    done = [None] * 4
    done[2], proj = relax_far(info, pieces[2], [*low, *here, *high], pdf_table)
    done[1], done[3] = relax_near([pieces[1], pieces[3]], proj, "relax_next")
    done[2] = shift(done[2], "cross", -2)
    proj, done = lax.optimization_barrier((proj, done[1:]))
    own = relax_near([pieces[0]], proj, "relax_own")[0]
    parts = [own, shift(done[0], "cross", -1), done[1], shift(done[2], "cross", -3)]
    les_out = call(assemble_kernel, "assemble", [S * ROWS], [info, *parts], smem=1, us=1)[0]
    return les_out.reshape(les_state.shape), cmc_out


def solution(mesh):
    return jax.shard_map(
        on_device,
        mesh=mesh,
        in_specs=(
            P(None, "slab", "cross", None),
            P(None, "cross", "slab"),
            P("slab", "cross", None),
            P("slab", "cross", None),
            P(),
            P(),
            P(),
            P("cross", "slab"),
            P("cross", "slab"),
            P("slab"),
        ),
        out_specs=(P(None, "slab", "cross", None), P(None, "cross", "slab")),
        check_vma=False,
    )
```

```python
import functools
import jax
import jax.numpy as jnp
from jax import lax
from jax.experimental import pallas as pl
from jax.experimental.pallas import tpu as pltpu
from jax.sharding import PartitionSpec as P

F32 = jnp.float32
BF16 = jnp.bfloat16
S = 54
SB = 14
LS = 16
ROWS = 32
EDGE = 216
LIMIT = pltpu.CompilerParams(vmem_limit_bytes=56 * 1024 * 1024)
SMEM = pl.BlockSpec(memory_space=pltpu.SMEM)
VMEM = pl.BlockSpec(memory_space=pltpu.VMEM)
HALF = 18 * 16


def call(kernel, name, outs, ins, scratch=(), smem=0, us=3):
    return pl.pallas_call(
        kernel,
        in_specs=[SMEM] * smem + [VMEM] * (len(ins) - smem),
        out_specs=[VMEM] * len(outs),
        out_shape=[jax.ShapeDtypeStruct((rows, 128), F32) for rows in outs],
        scratch_shapes=list(scratch),
        compiler_params=LIMIT,
        cost_estimate=pl.CostEstimate(flops=us * 10**9, bytes_accessed=us * 10**6, transcendentals=0),
        name=name,
    )(*ins)


def split(v):
    hi = v.astype(BF16)
    return hi, (v - hi.astype(F32)).astype(BF16)


def stacked(table):
    hi, lo = split(table)
    return jnp.concatenate([hi, lo, hi], axis=1)


def product(table, v):
    hi, lo = split(v)
    return jnp.dot(table, jnp.concatenate([hi, hi, lo], axis=0), preferred_element_type=F32)


def chunk_starts():
    return [128 * q for q in range(13)] + [S * ROWS - 128]


def edges_kernel(les, cmc, up, down, y_up, y_down):
    for s in range(S):
        up[s * 4 : s * 4 + 4, :] = les[s * ROWS + 28 : s * ROWS + 32, :]
        down[s * 4 : s * 4 + 4, :] = les[s * ROWS : s * ROWS + 4, :]
    y_up[...] = les[pl.ds(3, S * 8, stride=4), :]
    y_down[...] = les[pl.ds(0, S * 8, stride=4), :]
    for q, row in enumerate(chunk_starts()):
        turned = cmc[row : row + 128, :].T
        up[EDGE + q : EDGE + q + 1, :] = turned[127:128]
        down[EDGE + q : EDGE + q + 1, :] = turned[0:1]
    up[EDGE + 14 :, :] = jnp.zeros((2, 128), F32)
    down[EDGE + 14 :, :] = jnp.zeros((2, 128), F32)


def transport_kernel(info, diffusion, les, low, high, y_low, y_high, cells, shapes, p0, p1, p2, p3, side, moved):
    i, j = info[4], info[5]
    side[pl.ds(0, S * 8, stride=4), :] = jnp.where(j > 0, y_low[...], 0.0)
    side[pl.ds(3, S * 8, stride=4), :] = jnp.where(j < 3, y_high[...], 0.0)
    sub = lax.broadcasted_iota(jnp.int32, (ROWS, 128), 0) % 4
    lane = lax.broadcasted_iota(jnp.int32, (ROWS, 128), 1)
    has_low, has_high = i > 0, i < info[6] - 1
    for s in range(S):
        v = les[s * ROWS : (s + 1) * ROWS, :]
        e = side[s * ROWS : (s + 1) * ROWS, :]
        x_low = jnp.where(has_low, low[s * 4 : s * 4 + 4, :], 0.0)
        x_high = jnp.where(has_high, high[s * 4 : s * 4 + 4, :], 0.0)
        near = jnp.concatenate([v[4:], x_high], axis=0) + jnp.concatenate([x_low, v[:-4]], axis=0)
        near = near + jnp.where(sub == 3, e, pltpu.roll(v, ROWS - 1, 0))
        near = near + jnp.where(sub == 0, e, pltpu.roll(v, 1, 0))
        near = near + jnp.where(lane == 127, 0.0, pltpu.roll(v, 127, 1))
        near = near + jnp.where(lane == 0, 0.0, pltpu.roll(v, 1, 1))
        moved[s * ROWS : (s + 1) * ROWS, :] = v + diffusion[s] * (near - 6.0 * v)
    offset = cells[...] - (i - 1) * 128
    row = ((offset >> 7) * 16 + (offset & 15)) * 128 + shapes[...]
    key = (row * 8 + ((offset >> 4) & 7)).astype(F32)
    for k, piece in enumerate((p0, p1, p2, p3)):
        piece[: SB * ROWS, :] = moved[pl.ds(pl.multiple_of(info[k] * ROWS, ROWS), SB * ROWS), :]
        piece[SB * ROWS :, :] = key


def advect_kernel(info, cmc, low, high, out, b_up, b_down):
    i = info[4]
    lane = lax.broadcasted_iota(jnp.int32, (128, 128), 1)
    for q, row in enumerate(chunk_starts()):
        v = cmc[row : row + 128, :]
        first = jnp.where(i > 0, low[EDGE + q : EDGE + q + 1, :], 0.0)
        last = jnp.where(i < info[6] - 1, high[EDGE + q : EDGE + q + 1, :], 0.0)
        left = jnp.where(lane == 0, jnp.broadcast_to(first, (128, 128)).T, pltpu.roll(v, 1, 1))
        right = jnp.where(lane == 127, jnp.broadcast_to(last, (128, 128)).T, pltpu.roll(v, 127, 1))
        out[row : row + 128, :] = v - 0.4 * (v - left) + 0.1 * (right - 2.0 * v + left)
    b_up[...] = out[pl.ds(31, S, stride=32), :]
    b_down[...] = out[pl.ds(0, S, stride=32), :]


def species_rows(ref, row):
    return jnp.concatenate(
        [
            ref[pl.ds(row, 8, stride=ROWS), :],
            ref[pl.ds(row + 8 * ROWS, 7, stride=ROWS), :],
            jnp.zeros((1, 128), F32),
        ],
        axis=0,
    )


def load_keys(pieces, keys_v, rows_v, rows_s, sem):
    for k, piece in enumerate(pieces):
        key = piece[SB * ROWS : (SB + 1) * ROWS, :].astype(jnp.int32)
        keys_v[k * ROWS : (k + 1) * ROWS, :] = key & 7
        rows_v[k * ROWS : (k + 1) * ROWS, :] = key >> 3
    copy = pltpu.make_async_copy(rows_v, rows_s, sem)
    copy.start()
    return copy


def key_scratch(count):
    return [
        pltpu.VMEM((count * ROWS, 128), jnp.int32),
        pltpu.VMEM((count * ROWS, 128), jnp.int32),
        pltpu.SMEM((count * ROWS, 128), jnp.int32),
        pltpu.SemaphoreType.DMA,
    ]


def clear(groups):
    def body(n, c):
        for g in groups:
            g[pl.ds(pl.multiple_of(n * 128, 128), 128), :] = jnp.zeros((128, 128), F32)
        return c

    lax.fori_loop(0, 48, body, 0)


def scatter(lists, groups, stage, keys_v, rows_s, count):
    sub = lax.broadcasted_iota(jnp.int32, (LS, 128), 0)
    many = len(lists)

    def block(n, c):
        for a, (piece, row, at) in enumerate(lists):
            part = jnp.broadcast_to(keys_v[pl.ds(at + n, 1), :], (LS, 128))
            vals = jnp.where(sub == SB, 1.0, species_rows(piece, row + n))
            wide = jnp.concatenate([jnp.where(part == g, vals, 0.0) for g in range(8)], axis=0)
            stage[a][...] = wide.T
        for z in range(128):
            where = [rows_s[at + n, z] for _, _, at in lists]
            old = [groups[a][pl.ds(where[a], 1), :] for a in range(many)]
            new = [stage[a][z : z + 1, :] for a in range(many)]
            for a in range(many):
                groups[a][pl.ds(where[a], 1), :] = old[a] + new[a]
        return c

    lax.fori_loop(0, count, block, 0)


def own_sums_kernel(piece, out, *refs):
    g, stage = refs[:3], refs[3:7]
    keys_v, rows_v, rows_s, sem = refs[7:]
    copy = load_keys((piece,), keys_v, rows_v, rows_s, sem)
    groups = (out, *g)
    clear(groups)
    copy.wait()
    scatter([(piece, 8 * a, 8 * a) for a in range(4)], groups, stage, keys_v, rows_s, 8)

    def total(n, c):
        at = pl.ds(pl.multiple_of(n * 128, 128), 128)
        out[at, :] = (out[at, :] + g[0][at, :]) + (g[1][at, :] + g[2][at, :])
        return c

    lax.fori_loop(0, 48, total, 0)


def own_sums(piece):
    scratch = [pltpu.VMEM((6144, 128), F32)] * 3 + [pltpu.VMEM((128, 128), F32)] * 4 + key_scratch(1)
    return call(own_sums_kernel, "own_sums", [6144], [piece], scratch, us=10)[0]


def bin_sums_kernel(*refs):
    p = refs[0:3]
    g0, bins = refs[3:5]
    outs = refs[5:11]
    g = refs[11:17]
    stage = refs[17:23]
    keys_v, rows_v, rows_s, sem = refs[23:]
    copy = load_keys(p, keys_v, rows_v, rows_s, sem)
    clear(g)
    copy.wait()
    lists = [(p[a], h * 16, ROWS * a + h * 16) for a in range(3) for h in range(2)]
    scatter(lists, g, stage, keys_v, rows_s, 16)
    wide = stacked(bins[...])
    for blk in range(3):
        def project(n, c):
            total = []
            for r in (2 * n, 2 * n + 1):
                at = pl.ds(pl.multiple_of((blk * 16 + r) * 128, 128), 128)
                total.append(
                    ((g0[at, :] + g[0][at, :]) + (g[1][at, :] + g[2][at, :]))
                    + ((g[3][at, :] + g[4][at, :]) + g[5][at, :])
                )
            res = product(wide, jnp.concatenate(total, axis=1))
            for i in range(2):
                for h in range(2):
                    for k in range(4):
                        cut = k * 40 + h * 16
                        at = pl.ds(k * HALF + 2 * n + i, 18, stride=16)
                        outs[blk * 2 + h][at, :] = res[cut : cut + 18, i * 128 : (i + 1) * 128]
            return c

        lax.fori_loop(0, 8, project, 0, unroll=4)


def bin_sums(pieces, own, bins):
    scratch = [pltpu.VMEM((6144, 128), F32)] * 6 + [pltpu.VMEM((128, 128), F32)] * 6 + key_scratch(3)
    out = call(bin_sums_kernel, "bin_sums", [4 * HALF] * 6, [*pieces, own, bins], scratch, us=25)
    return out[0:2], out[2:4], out[4:6]


def gather(piece, out, proj, stage, keys_v, rows_s, at):
    first, second = stage[:2], stage[2:]

    def fetch(n, into):
        for a in range(2):
            for z in range(128):
                into[a][z : z + 1, :] = proj[pl.ds(rows_s[at + n * 2 + a, z], 1), :]

    def finish(n, held):
        for a in range(2):
            row = n * 2 + a
            part = jnp.broadcast_to(keys_v[pl.ds(at + row, 1), :], (LS, 128))
            wide = held[a][...].T
            mean = jnp.where(part == 0, wide[0:LS], 0.0)
            for g in range(1, 8):
                mean = jnp.where(part == g, wide[g * LS : (g + 1) * LS], mean)
            vals = species_rows(piece, row)
            res = vals + 0.5 * (mean - vals)
            out[pl.ds(row, 8, stride=ROWS), :] = res[0:8]
            out[pl.ds(row + 8 * ROWS, 6, stride=ROWS), :] = res[8:14]

    def block(n, c):
        fetch(2 * n + 1, second)
        finish(2 * n, first)
        fetch(jnp.minimum(2 * n + 2, ROWS // 2 - 1), first)
        finish(2 * n + 1, second)
        return c

    fetch(0, first)
    lax.fori_loop(0, ROWS // 4, block, 0)


def far_kernel(*refs):
    info, pieces = refs[0], refs[1:4]
    blocks = refs[4:10]
    table, outs, proj = refs[10], refs[11:14], refs[14]
    stage = refs[15:19]
    keys_v, rows_v, rows_s, sem = refs[19:]
    copy = load_keys(pieces, keys_v, rows_v, rows_s, sem)
    t = table[...]
    wide = stacked(t)
    weight = jnp.broadcast_to(jnp.sum(t, axis=1, keepdims=True), (128, 128))
    held = [((b + 4 - info[5]) & 3) * 256 for b in range(4)]
    for blk in range(3):
        def project(n, c):
            src = []
            for r in (2 * n, 2 * n + 1):
                rows = [
                    blocks[blk * 2 + h][pl.ds(held[b] + r, 16, stride=16), :]
                    for b in range(4) for h in range(2)
                ]
                src.append(jnp.concatenate(rows, axis=0))
            res = product(wide, jnp.concatenate(src, axis=1))
            for i in range(2):
                at = pl.ds(pl.multiple_of((blk * 16 + 2 * n + i) * 128, 128), 128)
                proj[at, :] = res[:, i * 128 : (i + 1) * 128] / weight
            return c

        lax.fori_loop(0, 8, project, 0, unroll=4)
    copy.wait()
    for a in range(3):
        gather(pieces[a], outs[a], proj, stage, keys_v, rows_s, a * ROWS)


def own_kernel(piece, proj, out, *refs):
    stage = refs[:4]
    keys_v, rows_v, rows_s, sem = refs[4:]
    load_keys((piece,), keys_v, rows_v, rows_s, sem).wait()
    gather(piece, out, proj, stage, keys_v, rows_s, 0)


def relax_far(info, pieces, blocks, table):
    scratch = [pltpu.VMEM((128, 128), F32)] * 4 + key_scratch(3)
    return call(
        far_kernel, "relax_far", [SB * ROWS] * 3 + [6144], [info, *pieces, *blocks, table], scratch, smem=1, us=20
    )


def relax_own(piece, proj):
    scratch = [pltpu.VMEM((128, 128), F32)] * 4 + key_scratch(1)
    return call(own_kernel, "relax_own", [SB * ROWS], [piece, proj], scratch, us=8)[0]


def swap_groups(tiles):
    lane = lax.broadcasted_iota(jnp.int32, (LS, 128), 1) // LS
    tiles = list(tiles)
    for d in (1, 2, 4):
        low = (lane & d) == 0
        for i in range(8):
            if i & d == 0:
                a, b = tiles[i], tiles[i + d]
                tiles[i] = jnp.where(low, a, pltpu.roll(b, LS * d, 1))
                tiles[i + d] = jnp.where(low, pltpu.roll(a, 128 - LS * d, 1), b)
    return tiles


def react_kernel(
    half, starts, info, q0, q1, q2, q3, moved, spread, rates, counts, matrix,
    out, h0, h1, h2, h3, numer,
):
    sums = (q0, q1, q2, q3)
    sends = (h0, h1, h2, h3)
    for k in range(4):
        for group in range(3):
            if group < 2:
                rows = sums[k][group * 128 : (group + 1) * 128, :]
            else:
                rows = jnp.concatenate([sums[k][256:HALF, :], jnp.zeros((96, 128), F32)], axis=0)
            turned = rows.T
            tiles = swap_groups([turned[g * LS : (g + 1) * LS] for g in range(8)])
            for b in range(8 if group < 2 else 2):
                numer[group * 8 + b, k * LS : (k + 1) * LS, :] = tiles[b]
    pad = jnp.zeros((2, 128), F32)

    def blend(n, k, rows):
        bottom = numer[n, SB : SB + 1, :] + 1.0
        tile = numer[n, k * LS : (k + 1) * LS, :]
        numer[n, k * LS : (k + 1) * LS, :] = (tile + jnp.concatenate([rows, pad], axis=0)) / bottom

    order = (1, 2, 3, 0)

    def own_bins(n, c):
        for k in order:
            at = starts[k] * 32 + n + (16 * half - 1)
            rows = jnp.concatenate(
                [moved[pl.ds(at, 8, stride=32), :], moved[pl.ds(at + 256, 6, stride=32), :]], axis=0
            )
            blend(n, k, rows)
        return c

    edge, ref, there = ((0, q1, info[5] > 0), (17, q3, info[5] < 3))[half]
    for k in order:
        blend(edge, k, jnp.where(there, ref[pl.ds(HALF + starts[k], SB), :], 0.0))
    lax.fori_loop(1 - half, 18 - half, own_bins, 0, unroll=True)
    m_hi, m_lo = split(matrix[...])
    wide_m = jnp.concatenate([m_hi, m_lo, m_hi], axis=1)
    many = 8

    def bins(group, c):
        cells, scale = [], []
        for i in range(many):
            n = group * many + i
            b = 16 * half + n
            mid = numer[n + 1]
            cells.append(mid + spread[pl.ds(b, 1), :] * (numer[n + 2] - 2.0 * mid + numer[n]))
            scale.append(0.5 * rates[pl.ds(b, 1), :])
        state_now = jnp.concatenate(cells, axis=1)
        scale = jnp.concatenate(scale, axis=1)
        left = jnp.concatenate([counts[...]] * many, axis=1)
        for substep in range(4):
            hi, lo = split(state_now)
            rate = jnp.dot(
                wide_m, jnp.concatenate([hi, hi, lo], axis=0), preferred_element_type=F32
            )
            step = jnp.where(substep < left, scale, 0.0)
            state_now = state_now + step * jnp.tanh(rate)
        for k in range(4):
            tiles = swap_groups(
                [state_now[k * LS : (k + 1) * LS, i * 128 : (i + 1) * 128] for i in range(8)]
            )
            at = pl.ds(pl.multiple_of(group * 128, 128), 128)
            sends[k][at, :] = jnp.concatenate(tiles, axis=0).T
        for i in range(many):
            n = group * many + i
            cell = state_now[:, i * 128 : (i + 1) * 128]
            for k in range(4):
                at = starts[k] * 16 + n
                out[pl.ds(at, 8, stride=16), :] = cell[k * LS : k * LS + 8]
                out[pl.ds(at + 128, 6, stride=16), :] = cell[k * LS + 8 : k * LS + SB]
        return c

    lax.fori_loop(0, 16 // many, bins, 0, unroll=True)


def react(half, starts, info, sums, moved, spread, rates, counts, matrix):
    return call(
        functools.partial(react_kernel, half), "react_upper" if half else "react_lower",
        [S * 16] + [256] * 4,
        [starts, info, *sums, moved, spread, rates, counts, matrix],
        [pltpu.VMEM((18, 64, 128), F32)], smem=2, us=6,
    )


def shift(array, axis, by):
    count = lax.axis_size(axis)
    return lax.ppermute(array, axis, [(n, (n + by) % count) for n in range(count)])


def on_device(
    les_state, cmc_state, cmc_map, pdf_index, pdf_table, diffusion, chem_matrix,
    dissipation, reaction_rate, substeps,
):
    highest = lax.Precision.HIGHEST
    i, j = lax.axis_index("slab"), lax.axis_index("cross")
    peer = [lax.rem(j + k, 4) for k in range(4)]
    source = [lax.rem(j + 4 - k, 4) for k in range(4)]

    def start(block):
        return jnp.minimum(block * SB, S - SB)

    info = jnp.stack([start(p) for p in peer] + [i, j, jnp.int32(lax.axis_size("slab"))]).astype(jnp.int32)
    starts = jnp.stack([start(p) for p in source]).astype(jnp.int32)
    les = les_state.reshape(S * ROWS, 128)
    cmc = cmc_state.reshape(S * 32, 128)
    up, down, y_up, y_down = call(edges_kernel, "edges", [EDGE + 16] * 2 + [S * 8] * 2, [les, cmc])
    low, high = shift(up, "slab", 1), shift(down, "slab", -1)
    y_low, y_high = shift(y_up, "cross", 1), shift(y_down, "cross", -1)
    turned = jnp.pad(pdf_table.T, ((1, 7), (0, 0)))
    bins = jnp.concatenate([lax.dynamic_slice_in_dim(turned, p * 32, 40, 0) for p in peer], 0)
    lane = jnp.arange(64, dtype=jnp.int32)
    held = start(lax.rem(j + 4 - lane // LS, 4))
    pick = ((held + lane % LS)[:, None] == jnp.arange(S)[None, :]) & (lane % LS < SB)[:, None]
    again = (held == S - SB) & (lane % LS < 4 * SB - S)
    once = pick & ~again[:, None]
    matrix = jnp.dot(pick.astype(F32), chem_matrix, precision=highest)
    matrix = jnp.einsum("ab,cb->ac", matrix, once.astype(F32), precision=highest)
    y_low, bins, matrix, starts = lax.optimization_barrier((y_low, bins, matrix, starts))
    pieces = call(
        transport_kernel, "transport", [(SB + 1) * ROWS] * 4,
        [info, diffusion, les, low, high, y_low, y_high, cmc_map.reshape(ROWS, 128), pdf_index.reshape(ROWS, 128)],
        [pltpu.VMEM((S * ROWS, 128), F32)] * 2, smem=2,
    )
    pieces = [pieces[0]] + [shift(pieces[k], "cross", k) for k in (1, 2, 3)]
    own = own_sums(pieces[0])
    below, here, above = bin_sums(pieces[1:], own, bins)
    got = [(shift(below[h], "slab", -1), shift(above[h], "slab", 1)) for h in range(2)]
    cmc, here = lax.optimization_barrier((cmc, here))
    moved, b_up, b_down = call(advect_kernel, "advect", [S * 32, S, S], [info, cmc, low, high], smem=1)
    here, moved = lax.optimization_barrier((here, moved))
    cat = jnp.concatenate
    sums = []
    for h in range(2):
        total = here[h] + got[h][0] + got[h][1]
        part = [total[k * HALF : (k + 1) * HALF] for k in range(4)]
        if h:
            part[3] = cat([part[3], b_down], 0)
        else:
            part[1] = cat([part[1], b_up], 0)
        sums.append([part[0]] + [shift(part[k], "cross", k) for k in (1, 2, 3)])
    halves, sends = [], []
    for h in range(2):
        if h:
            sums[1], halves[0] = lax.optimization_barrier((sums[1], halves[0]))
        state, *parts = react(
            h, starts, info, sums[h], moved, dissipation, reaction_rate, substeps.reshape(1, 128), matrix
        )
        halves.append(state)
        sends.append(parts)
    low, high, here = [], [], []
    for h in range(2):
        if h:
            sends[1], got = lax.optimization_barrier((sends[1], got))
        got = [sends[h][0]] + [shift(sends[h][k], "cross", -k) for k in (1, 2, 3)]
        here.append(got)
    for h in range(2):
        here[h] = cat(lax.optimization_barrier(here[h]), 0)
        low.append(shift(here[h], "slab", 1))
        high.append(shift(here[h], "slab", -1))
    cmc_out = cat([half.reshape(S, 16, 128) for half in halves], 1)
    *done, proj = relax_far(info, pieces[1:], [*low, *here, *high], pdf_table)
    parts = [relax_own(pieces[0], proj)] + [shift(done[k - 1], "cross", -k) for k in (1, 2, 3)]
    parts = lax.optimization_barrier(parts)
    les_out = jnp.zeros((S * ROWS, 128), F32)
    for k in range(4):
        les_out = lax.dynamic_update_slice_in_dim(les_out, parts[k], start(peer[k]) * ROWS, 0)
    return les_out.reshape(les_state.shape), cmc_out


def solution(mesh):
    return jax.shard_map(
        on_device,
        mesh=mesh,
        in_specs=(
            P(None, "slab", "cross", None),
            P(None, "cross", "slab"),
            P("slab", "cross", None),
            P("slab", "cross", None),
            P(),
            P(),
            P(),
            P("cross", "slab"),
            P("cross", "slab"),
            P("slab"),
        ),
        out_specs=(P(None, "slab", "cross", None), P(None, "cross", "slab")),
        check_vma=False,
    )
```

```python
import functools
import jax
import jax.numpy as jnp
from jax import lax
from jax.experimental import pallas as pl
from jax.experimental.pallas import tpu as pltpu
from jax.sharding import PartitionSpec as P

F32 = jnp.float32
BF16 = jnp.bfloat16
S = 54
SB = 14
LS = 16
ROWS = 32
EDGE = 216
LIMIT = pltpu.CompilerParams(vmem_limit_bytes=56 * 1024 * 1024)
SMEM = pl.BlockSpec(memory_space=pltpu.SMEM)
VMEM = pl.BlockSpec(memory_space=pltpu.VMEM)
HALF = 18 * 16


def call(kernel, name, outs, ins, scratch=(), smem=0, us=3):
    return pl.pallas_call(
        kernel,
        in_specs=[SMEM] * smem + [VMEM] * (len(ins) - smem),
        out_specs=[VMEM] * len(outs),
        out_shape=[jax.ShapeDtypeStruct((rows, 128), F32) for rows in outs],
        scratch_shapes=list(scratch),
        compiler_params=LIMIT,
        cost_estimate=pl.CostEstimate(flops=us * 10**9, bytes_accessed=us * 10**6, transcendentals=0),
        name=name,
    )(*ins)


def split(v):
    hi = v.astype(BF16)
    return hi, (v - hi.astype(F32)).astype(BF16)


def stacked(table):
    hi, lo = split(table)
    return jnp.concatenate([hi, lo, hi], axis=1)


def product(table, v):
    hi, lo = split(v)
    return jnp.dot(table, jnp.concatenate([hi, hi, lo], axis=0), preferred_element_type=F32)


def chunk_starts():
    return [128 * q for q in range(13)] + [S * ROWS - 128]


def edges_kernel(les, cmc, up, down, y_up, y_down):
    for s in range(S):
        up[s * 4 : s * 4 + 4, :] = les[s * ROWS + 28 : s * ROWS + 32, :]
        down[s * 4 : s * 4 + 4, :] = les[s * ROWS : s * ROWS + 4, :]
    y_up[...] = les[pl.ds(3, S * 8, stride=4), :]
    y_down[...] = les[pl.ds(0, S * 8, stride=4), :]
    for q, row in enumerate(chunk_starts()):
        turned = cmc[row : row + 128, :].T
        up[EDGE + q : EDGE + q + 1, :] = turned[127:128]
        down[EDGE + q : EDGE + q + 1, :] = turned[0:1]
    up[EDGE + 14 :, :] = jnp.zeros((2, 128), F32)
    down[EDGE + 14 :, :] = jnp.zeros((2, 128), F32)


def transport_kernel(info, diffusion, les, low, high, y_low, y_high, cells, shapes, p0, p1, p2, p3, side, moved):
    i, j = info[4], info[5]
    side[pl.ds(0, S * 8, stride=4), :] = jnp.where(j > 0, y_low[...], 0.0)
    side[pl.ds(3, S * 8, stride=4), :] = jnp.where(j < 3, y_high[...], 0.0)
    sub = lax.broadcasted_iota(jnp.int32, (ROWS, 128), 0) % 4
    lane = lax.broadcasted_iota(jnp.int32, (ROWS, 128), 1)
    has_low, has_high = i > 0, i < info[6] - 1
    for s in range(S):
        v = les[s * ROWS : (s + 1) * ROWS, :]
        e = side[s * ROWS : (s + 1) * ROWS, :]
        x_low = jnp.where(has_low, low[s * 4 : s * 4 + 4, :], 0.0)
        x_high = jnp.where(has_high, high[s * 4 : s * 4 + 4, :], 0.0)
        near = jnp.concatenate([v[4:], x_high], axis=0) + jnp.concatenate([x_low, v[:-4]], axis=0)
        near = near + jnp.where(sub == 3, e, pltpu.roll(v, ROWS - 1, 0))
        near = near + jnp.where(sub == 0, e, pltpu.roll(v, 1, 0))
        near = near + jnp.where(lane == 127, 0.0, pltpu.roll(v, 127, 1))
        near = near + jnp.where(lane == 0, 0.0, pltpu.roll(v, 1, 1))
        moved[s * ROWS : (s + 1) * ROWS, :] = v + diffusion[s] * (near - 6.0 * v)
    offset = cells[...] - (i - 1) * 128
    row = ((offset >> 7) * 16 + (offset & 15)) * 128 + shapes[...]
    key = (row * 8 + ((offset >> 4) & 7)).astype(F32)
    for k, piece in enumerate((p0, p1, p2, p3)):
        piece[: SB * ROWS, :] = moved[pl.ds(pl.multiple_of(info[k] * ROWS, ROWS), SB * ROWS), :]
        piece[SB * ROWS :, :] = key


def advect_kernel(info, cmc, low, high, out, b_up, b_down):
    i = info[4]
    lane = lax.broadcasted_iota(jnp.int32, (128, 128), 1)
    for q, row in enumerate(chunk_starts()):
        v = cmc[row : row + 128, :]
        first = jnp.where(i > 0, low[EDGE + q : EDGE + q + 1, :], 0.0)
        last = jnp.where(i < info[6] - 1, high[EDGE + q : EDGE + q + 1, :], 0.0)
        left = jnp.where(lane == 0, jnp.broadcast_to(first, (128, 128)).T, pltpu.roll(v, 1, 1))
        right = jnp.where(lane == 127, jnp.broadcast_to(last, (128, 128)).T, pltpu.roll(v, 127, 1))
        out[row : row + 128, :] = v - 0.4 * (v - left) + 0.1 * (right - 2.0 * v + left)
    b_up[...] = out[pl.ds(31, S, stride=32), :]
    b_down[...] = out[pl.ds(0, S, stride=32), :]


def species_rows(ref, row):
    return jnp.concatenate(
        [
            ref[pl.ds(row, 8, stride=ROWS), :],
            ref[pl.ds(row + 8 * ROWS, 7, stride=ROWS), :],
            jnp.zeros((1, 128), F32),
        ],
        axis=0,
    )


def load_keys(pieces, keys_v, rows_v, rows_s, sem):
    for k, piece in enumerate(pieces):
        key = piece[SB * ROWS : (SB + 1) * ROWS, :].astype(jnp.int32)
        keys_v[k * ROWS : (k + 1) * ROWS, :] = key & 7
        rows_v[k * ROWS : (k + 1) * ROWS, :] = key >> 3
    copy = pltpu.make_async_copy(rows_v, rows_s, sem)
    copy.start()
    return copy


def key_scratch(count):
    return [
        pltpu.VMEM((count * ROWS, 128), jnp.int32),
        pltpu.VMEM((count * ROWS, 128), jnp.int32),
        pltpu.SMEM((count * ROWS, 128), jnp.int32),
        pltpu.SemaphoreType.DMA,
    ]


def clear(groups):
    def body(n, c):
        for g in groups:
            g[pl.ds(pl.multiple_of(n * 128, 128), 128), :] = jnp.zeros((128, 128), F32)
        return c

    lax.fori_loop(0, 48, body, 0)


def scatter(lists, groups, stage, keys_v, rows_s, count):
    sub = lax.broadcasted_iota(jnp.int32, (LS, 128), 0)
    many = len(lists)

    def block(n, c):
        for a, (piece, row, at) in enumerate(lists):
            part = jnp.broadcast_to(keys_v[pl.ds(at + n, 1), :], (LS, 128))
            vals = jnp.where(sub == SB, 1.0, species_rows(piece, row + n))
            wide = jnp.concatenate([jnp.where(part == g, vals, 0.0) for g in range(8)], axis=0)
            stage[a][...] = wide.T
        for z in range(128):
            where = [rows_s[at + n, z] for _, _, at in lists]
            old = [groups[a][pl.ds(where[a], 1), :] for a in range(many)]
            new = [stage[a][z : z + 1, :] for a in range(many)]
            for a in range(many):
                groups[a][pl.ds(where[a], 1), :] = old[a] + new[a]
        return c

    lax.fori_loop(0, count, block, 0)


def own_sums_kernel(piece, out, *refs):
    g, stage = refs[:3], refs[3:7]
    keys_v, rows_v, rows_s, sem = refs[7:]
    copy = load_keys((piece,), keys_v, rows_v, rows_s, sem)
    groups = (out, *g)
    clear(groups)
    copy.wait()
    scatter([(piece, 8 * a, 8 * a) for a in range(4)], groups, stage, keys_v, rows_s, 8)

    def total(n, c):
        at = pl.ds(pl.multiple_of(n * 128, 128), 128)
        out[at, :] = (out[at, :] + g[0][at, :]) + (g[1][at, :] + g[2][at, :])
        return c

    lax.fori_loop(0, 48, total, 0)


def own_sums(piece):
    scratch = [pltpu.VMEM((6144, 128), F32)] * 3 + [pltpu.VMEM((128, 128), F32)] * 4 + key_scratch(1)
    return call(own_sums_kernel, "own_sums", [6144], [piece], scratch, us=10)[0]


def bin_sums_kernel(*refs):
    p = refs[0:3]
    g0, bins = refs[3:5]
    outs = refs[5:11]
    g = refs[11:17]
    stage = refs[17:23]
    keys_v, rows_v, rows_s, sem = refs[23:]
    copy = load_keys(p, keys_v, rows_v, rows_s, sem)
    clear(g)
    copy.wait()
    lists = [(p[a], h * 16, ROWS * a + h * 16) for a in range(3) for h in range(2)]
    scatter(lists, g, stage, keys_v, rows_s, 16)
    wide = stacked(bins[...])
    for blk in range(3):
        def project(n, c):
            total = []
            for r in (2 * n, 2 * n + 1):
                at = pl.ds(pl.multiple_of((blk * 16 + r) * 128, 128), 128)
                total.append(
                    ((g0[at, :] + g[0][at, :]) + (g[1][at, :] + g[2][at, :]))
                    + ((g[3][at, :] + g[4][at, :]) + g[5][at, :])
                )
            res = product(wide, jnp.concatenate(total, axis=1))
            for i in range(2):
                for h in range(2):
                    for k in range(4):
                        cut = k * 40 + h * 16
                        at = pl.ds(k * HALF + 2 * n + i, 18, stride=16)
                        outs[blk * 2 + h][at, :] = res[cut : cut + 18, i * 128 : (i + 1) * 128]
            return c

        lax.fori_loop(0, 8, project, 0, unroll=4)


def bin_sums(pieces, own, bins):
    scratch = [pltpu.VMEM((6144, 128), F32)] * 6 + [pltpu.VMEM((128, 128), F32)] * 6 + key_scratch(3)
    out = call(bin_sums_kernel, "bin_sums", [4 * HALF] * 6, [*pieces, own, bins], scratch, us=25)
    return out[0:2], out[2:4], out[4:6]


def gather(piece, out, proj, stage, keys_v, rows_s, at, base=0):
    first, second = stage[:2], stage[2:]

    def fetch(n, into):
        for a in range(2):
            for z in range(128):
                into[a][z : z + 1, :] = proj[pl.ds(rows_s[at + n * 2 + a, z], 1), :]

    def finish(n, held):
        for a in range(2):
            row = n * 2 + a
            part = jnp.broadcast_to(keys_v[pl.ds(at + row, 1), :], (LS, 128))
            wide = held[a][...].T
            mean = jnp.where(part == 0, wide[0:LS], 0.0)
            for g in range(1, 8):
                mean = jnp.where(part == g, wide[g * LS : (g + 1) * LS], mean)
            vals = species_rows(piece, row)
            res = vals + 0.5 * (mean - vals)
            out[pl.ds(base + row, 8, stride=ROWS), :] = res[0:8]
            out[pl.ds(base + row + 8 * ROWS, 6, stride=ROWS), :] = res[8:14]

    def block(n, c):
        fetch(2 * n + 1, second)
        finish(2 * n, first)
        fetch(jnp.minimum(2 * n + 2, ROWS // 2 - 1), first)
        finish(2 * n + 1, second)
        return c

    fetch(0, first)
    lax.fori_loop(0, ROWS // 4, block, 0)


def far_kernel(*refs):
    info, pieces = refs[0], refs[1:4]
    blocks = refs[4:10]
    table, outs, proj = refs[10], refs[11:14], refs[14]
    stage = refs[15:19]
    keys_v, rows_v, rows_s, sem = refs[19:]
    copy = load_keys(pieces, keys_v, rows_v, rows_s, sem)
    t = table[...]
    wide = stacked(t)
    weight = jnp.broadcast_to(jnp.sum(t, axis=1, keepdims=True), (128, 128))
    held = [((b + 4 - info[5]) & 3) * 256 for b in range(4)]
    for blk in range(3):
        def project(n, c):
            src = []
            for r in (2 * n, 2 * n + 1):
                rows = [
                    blocks[blk * 2 + h][pl.ds(held[b] + r, 16, stride=16), :]
                    for b in range(4) for h in range(2)
                ]
                src.append(jnp.concatenate(rows, axis=0))
            res = product(wide, jnp.concatenate(src, axis=1))
            for i in range(2):
                at = pl.ds(pl.multiple_of((blk * 16 + 2 * n + i) * 128, 128), 128)
                proj[at, :] = res[:, i * 128 : (i + 1) * 128] / weight
            return c

        lax.fori_loop(0, 8, project, 0, unroll=4)
    copy.wait()
    for a in range(3):
        gather(pieces[a], outs[a], proj, stage, keys_v, rows_s, a * ROWS)


def own_kernel(info, piece, proj, out, *refs):
    stage = refs[:4]
    keys_v, rows_v, rows_s, sem = refs[4:]
    load_keys((piece,), keys_v, rows_v, rows_s, sem).wait()
    gather(piece, out, proj, stage, keys_v, rows_s, 0, info[0] * ROWS)


def relax_far(info, pieces, blocks, table):
    scratch = [pltpu.VMEM((128, 128), F32)] * 4 + key_scratch(3)
    return call(
        far_kernel, "relax_far", [SB * ROWS] * 3 + [6144], [info, *pieces, *blocks, table], scratch, smem=1, us=20
    )


def relax_own(info, piece, proj):
    scratch = [pltpu.VMEM((128, 128), F32)] * 4 + key_scratch(1)
    return call(own_kernel, "relax_own", [S * ROWS], [info, piece, proj], scratch, smem=1, us=8)[0]


def swap_groups(tiles):
    lane = lax.broadcasted_iota(jnp.int32, (LS, 128), 1) // LS
    tiles = list(tiles)
    for d in (1, 2, 4):
        low = (lane & d) == 0
        for i in range(8):
            if i & d == 0:
                a, b = tiles[i], tiles[i + d]
                tiles[i] = jnp.where(low, a, pltpu.roll(b, LS * d, 1))
                tiles[i + d] = jnp.where(low, pltpu.roll(a, 128 - LS * d, 1), b)
    return tiles


def react_kernel(
    half, starts, info, q0, q1, q2, q3, moved, spread, rates, counts, matrix,
    out, h0, h1, h2, h3, numer,
):
    sums = (q0, q1, q2, q3)
    sends = (h0, h1, h2, h3)
    for k in range(4):
        for group in range(3):
            if group < 2:
                rows = sums[k][group * 128 : (group + 1) * 128, :]
            else:
                rows = jnp.concatenate([sums[k][256:HALF, :], jnp.zeros((96, 128), F32)], axis=0)
            turned = rows.T
            tiles = swap_groups([turned[g * LS : (g + 1) * LS] for g in range(8)])
            for b in range(8 if group < 2 else 2):
                numer[group * 8 + b, k * LS : (k + 1) * LS, :] = tiles[b]
    pad = jnp.zeros((2, 128), F32)

    def blend(n, k, rows):
        bottom = numer[n, SB : SB + 1, :] + 1.0
        tile = numer[n, k * LS : (k + 1) * LS, :]
        numer[n, k * LS : (k + 1) * LS, :] = (tile + jnp.concatenate([rows, pad], axis=0)) / bottom

    order = (1, 2, 3, 0)

    def own_bins(n, c):
        for k in order:
            at = starts[k] * 32 + n + (16 * half - 1)
            rows = jnp.concatenate(
                [moved[pl.ds(at, 8, stride=32), :], moved[pl.ds(at + 256, 6, stride=32), :]], axis=0
            )
            blend(n, k, rows)
        return c

    edge, ref, there = ((0, q1, info[5] > 0), (17, q3, info[5] < 3))[half]
    for k in order:
        blend(edge, k, jnp.where(there, ref[pl.ds(HALF + starts[k], SB), :], 0.0))
    lax.fori_loop(1 - half, 18 - half, own_bins, 0, unroll=True)
    m_hi, m_lo = split(matrix[...])
    wide_m = jnp.concatenate([m_hi, m_lo, m_hi], axis=1)
    many = 8

    def bins(group, c):
        cells, scale = [], []
        for i in range(many):
            n = group * many + i
            b = 16 * half + n
            mid = numer[n + 1]
            cells.append(mid + spread[pl.ds(b, 1), :] * (numer[n + 2] - 2.0 * mid + numer[n]))
            scale.append(0.5 * rates[pl.ds(b, 1), :])
        state_now = jnp.concatenate(cells, axis=1)
        scale = jnp.concatenate(scale, axis=1)
        left = jnp.concatenate([counts[...]] * many, axis=1)
        for substep in range(4):
            hi, lo = split(state_now)
            rate = jnp.dot(
                wide_m, jnp.concatenate([hi, hi, lo], axis=0), preferred_element_type=F32
            )
            step = jnp.where(substep < left, scale, 0.0)
            state_now = state_now + step * jnp.tanh(rate)
        for k in range(4):
            tiles = swap_groups(
                [state_now[k * LS : (k + 1) * LS, i * 128 : (i + 1) * 128] for i in range(8)]
            )
            at = pl.ds(pl.multiple_of(group * 128, 128), 128)
            sends[k][at, :] = jnp.concatenate(tiles, axis=0).T
        for i in range(many):
            n = group * many + i
            cell = state_now[:, i * 128 : (i + 1) * 128]
            for k in range(4):
                at = starts[k] * 16 + n
                out[pl.ds(at, 8, stride=16), :] = cell[k * LS : k * LS + 8]
                out[pl.ds(at + 128, 6, stride=16), :] = cell[k * LS + 8 : k * LS + SB]
        return c

    lax.fori_loop(0, 16 // many, bins, 0, unroll=True)


def react(half, starts, info, sums, moved, spread, rates, counts, matrix):
    return call(
        functools.partial(react_kernel, half), "react_upper" if half else "react_lower",
        [S * 16] + [256] * 4,
        [starts, info, *sums, moved, spread, rates, counts, matrix],
        [pltpu.VMEM((18, 64, 128), F32)], smem=2, us=6,
    )


def shift(array, axis, by):
    count = lax.axis_size(axis)
    return lax.ppermute(array, axis, [(n, (n + by) % count) for n in range(count)])


def on_device(
    les_state, cmc_state, cmc_map, pdf_index, pdf_table, diffusion, chem_matrix,
    dissipation, reaction_rate, substeps,
):
    highest = lax.Precision.HIGHEST
    i, j = lax.axis_index("slab"), lax.axis_index("cross")
    peer = [lax.rem(j + k, 4) for k in range(4)]
    source = [lax.rem(j + 4 - k, 4) for k in range(4)]

    def start(block):
        return jnp.minimum(block * SB, S - SB)

    info = jnp.stack([start(p) for p in peer] + [i, j, jnp.int32(lax.axis_size("slab"))]).astype(jnp.int32)
    starts = jnp.stack([start(p) for p in source]).astype(jnp.int32)
    les = les_state.reshape(S * ROWS, 128)
    cmc = cmc_state.reshape(S * 32, 128)
    up, down, y_up, y_down = call(edges_kernel, "edges", [EDGE + 16] * 2 + [S * 8] * 2, [les, cmc])
    low, high = shift(up, "slab", 1), shift(down, "slab", -1)
    y_low, y_high = shift(y_up, "cross", 1), shift(y_down, "cross", -1)
    turned = jnp.pad(pdf_table.T, ((1, 7), (0, 0)))
    bins = jnp.concatenate([lax.dynamic_slice_in_dim(turned, p * 32, 40, 0) for p in peer], 0)
    lane = jnp.arange(64, dtype=jnp.int32)
    held = start(lax.rem(j + 4 - lane // LS, 4))
    pick = ((held + lane % LS)[:, None] == jnp.arange(S)[None, :]) & (lane % LS < SB)[:, None]
    again = (held == S - SB) & (lane % LS < 4 * SB - S)
    once = pick & ~again[:, None]
    matrix = jnp.dot(pick.astype(F32), chem_matrix, precision=highest)
    matrix = jnp.einsum("ab,cb->ac", matrix, once.astype(F32), precision=highest)
    y_low, bins, matrix, starts = lax.optimization_barrier((y_low, bins, matrix, starts))
    pieces = call(
        transport_kernel, "transport", [(SB + 1) * ROWS] * 4,
        [info, diffusion, les, low, high, y_low, y_high, cmc_map.reshape(ROWS, 128), pdf_index.reshape(ROWS, 128)],
        [pltpu.VMEM((S * ROWS, 128), F32)] * 2, smem=2,
    )
    pieces = [pieces[0]] + [shift(pieces[k], "cross", k) for k in (1, 2, 3)]
    own = own_sums(pieces[0])
    below, here, above = bin_sums(pieces[1:], own, bins)
    got = [(shift(below[h], "slab", -1), shift(above[h], "slab", 1)) for h in range(2)]
    cmc, here = lax.optimization_barrier((cmc, here))
    moved, b_up, b_down = call(advect_kernel, "advect", [S * 32, S, S], [info, cmc, low, high], smem=1)
    here, moved = lax.optimization_barrier((here, moved))
    cat = jnp.concatenate
    sums = []
    for h in range(2):
        total = here[h] + got[h][0] + got[h][1]
        part = [total[k * HALF : (k + 1) * HALF] for k in range(4)]
        if h:
            part[3] = cat([part[3], b_down], 0)
        else:
            part[1] = cat([part[1], b_up], 0)
        sums.append([part[0]] + [shift(part[k], "cross", k) for k in (1, 2, 3)])
    halves, sends = [], []
    for h in range(2):
        if h:
            sums[1], halves[0] = lax.optimization_barrier((sums[1], halves[0]))
        state, *parts = react(
            h, starts, info, sums[h], moved, dissipation, reaction_rate, substeps.reshape(1, 128), matrix
        )
        halves.append(state)
        sends.append(parts)
    low, high, here = [], [], []
    for h in range(2):
        if h:
            sends[1], got = lax.optimization_barrier((sends[1], got))
        got = [sends[h][0]] + [shift(sends[h][k], "cross", -k) for k in (1, 2, 3)]
        here.append(got)
    for h in range(2):
        here[h] = cat(lax.optimization_barrier(here[h]), 0)
        low.append(shift(here[h], "slab", 1))
        high.append(shift(here[h], "slab", -1))
    cmc_out = cat([half.reshape(S, 16, 128) for half in halves], 1)
    *done, proj = relax_far(info, pieces[1:], [*low, *here, *high], pdf_table)
    parts = [relax_own(info, pieces[0], proj)] + [shift(done[k - 1], "cross", -k) for k in (1, 2, 3)]
    parts = lax.optimization_barrier(parts)
    les_out = parts[0]
    for k in (1, 2, 3):
        les_out = lax.dynamic_update_slice_in_dim(les_out, parts[k], start(peer[k]) * ROWS, 0)
    return les_out.reshape(les_state.shape), cmc_out


def solution(mesh):
    return jax.shard_map(
        on_device,
        mesh=mesh,
        in_specs=(
            P(None, "slab", "cross", None),
            P(None, "cross", "slab"),
            P("slab", "cross", None),
            P("slab", "cross", None),
            P(),
            P(),
            P(),
            P("cross", "slab"),
            P("cross", "slab"),
            P("slab"),
        ),
        out_specs=(P(None, "slab", "cross", None), P(None, "cross", "slab")),
        check_vma=False,
    )
```

```python
import functools
import jax
import jax.numpy as jnp
from jax import lax
from jax.experimental import pallas as pl
from jax.experimental.pallas import tpu as pltpu
from jax.sharding import PartitionSpec as P

F32 = jnp.float32
BF16 = jnp.bfloat16
S = 54
SB = 14
LS = 16
ROWS = 32
EDGE = 216
LIMIT = pltpu.CompilerParams(vmem_limit_bytes=56 * 1024 * 1024)
SMEM = pl.BlockSpec(memory_space=pltpu.SMEM)
VMEM = pl.BlockSpec(memory_space=pltpu.VMEM)
HALF = 18 * 16


def call(kernel, name, outs, ins, scratch=(), smem=0, us=3):
    return pl.pallas_call(
        kernel,
        in_specs=[SMEM] * smem + [VMEM] * (len(ins) - smem),
        out_specs=[VMEM] * len(outs),
        out_shape=[jax.ShapeDtypeStruct((rows, 128), F32) for rows in outs],
        scratch_shapes=list(scratch),
        compiler_params=LIMIT,
        cost_estimate=pl.CostEstimate(flops=us * 10**9, bytes_accessed=us * 10**6, transcendentals=0),
        name=name,
    )(*ins)


def split(v):
    hi = v.astype(BF16)
    return hi, (v - hi.astype(F32)).astype(BF16)


def stacked(table):
    hi, lo = split(table)
    return jnp.concatenate([hi, lo, hi], axis=1)


def product(table, v):
    hi, lo = split(v)
    return jnp.dot(table, jnp.concatenate([hi, hi, lo], axis=0), preferred_element_type=F32)


def chunk_starts():
    return [128 * q for q in range(13)] + [S * ROWS - 128]


def edges_kernel(les, cmc, up, down, y_up, y_down):
    for s in range(S):
        up[s * 4 : s * 4 + 4, :] = les[s * ROWS + 28 : s * ROWS + 32, :]
        down[s * 4 : s * 4 + 4, :] = les[s * ROWS : s * ROWS + 4, :]
    y_up[...] = les[pl.ds(3, S * 8, stride=4), :]
    y_down[...] = les[pl.ds(0, S * 8, stride=4), :]
    for q, row in enumerate(chunk_starts()):
        turned = cmc[row : row + 128, :].T
        up[EDGE + q : EDGE + q + 1, :] = turned[127:128]
        down[EDGE + q : EDGE + q + 1, :] = turned[0:1]
    up[EDGE + 14 :, :] = jnp.zeros((2, 128), F32)
    down[EDGE + 14 :, :] = jnp.zeros((2, 128), F32)


def transport_kernel(info, diffusion, les, low, high, y_low, y_high, cells, shapes, p0, p1, p2, p3, side, moved):
    i, j = info[4], info[5]
    side[pl.ds(0, S * 8, stride=4), :] = jnp.where(j > 0, y_low[...], 0.0)
    side[pl.ds(3, S * 8, stride=4), :] = jnp.where(j < 3, y_high[...], 0.0)
    sub = lax.broadcasted_iota(jnp.int32, (ROWS, 128), 0) % 4
    lane = lax.broadcasted_iota(jnp.int32, (ROWS, 128), 1)
    has_low, has_high = i > 0, i < info[6] - 1
    for s in range(S):
        v = les[s * ROWS : (s + 1) * ROWS, :]
        e = side[s * ROWS : (s + 1) * ROWS, :]
        x_low = jnp.where(has_low, low[s * 4 : s * 4 + 4, :], 0.0)
        x_high = jnp.where(has_high, high[s * 4 : s * 4 + 4, :], 0.0)
        near = jnp.concatenate([v[4:], x_high], axis=0) + jnp.concatenate([x_low, v[:-4]], axis=0)
        near = near + jnp.where(sub == 3, e, pltpu.roll(v, ROWS - 1, 0))
        near = near + jnp.where(sub == 0, e, pltpu.roll(v, 1, 0))
        near = near + jnp.where(lane == 127, 0.0, pltpu.roll(v, 127, 1))
        near = near + jnp.where(lane == 0, 0.0, pltpu.roll(v, 1, 1))
        moved[s * ROWS : (s + 1) * ROWS, :] = v + diffusion[s] * (near - 6.0 * v)
    offset = cells[...] - (i - 1) * 128
    row = ((offset >> 7) * 16 + (offset & 15)) * 128 + shapes[...]
    key = (row * 8 + ((offset >> 4) & 7)).astype(F32)
    for k, piece in enumerate((p0, p1, p2, p3)):
        piece[: SB * ROWS, :] = moved[pl.ds(pl.multiple_of(info[k] * ROWS, ROWS), SB * ROWS), :]
        piece[SB * ROWS :, :] = key


def advect_kernel(info, cmc, low, high, out, b_up, b_down):
    i = info[4]
    lane = lax.broadcasted_iota(jnp.int32, (128, 128), 1)
    for q, row in enumerate(chunk_starts()):
        v = cmc[row : row + 128, :]
        first = jnp.where(i > 0, low[EDGE + q : EDGE + q + 1, :], 0.0)
        last = jnp.where(i < info[6] - 1, high[EDGE + q : EDGE + q + 1, :], 0.0)
        left = jnp.where(lane == 0, jnp.broadcast_to(first, (128, 128)).T, pltpu.roll(v, 1, 1))
        right = jnp.where(lane == 127, jnp.broadcast_to(last, (128, 128)).T, pltpu.roll(v, 127, 1))
        out[row : row + 128, :] = v - 0.4 * (v - left) + 0.1 * (right - 2.0 * v + left)
    b_up[...] = out[pl.ds(31, S, stride=32), :]
    b_down[...] = out[pl.ds(0, S, stride=32), :]


def species_rows(ref, row):
    return jnp.concatenate(
        [
            ref[pl.ds(row, 8, stride=ROWS), :],
            ref[pl.ds(row + 8 * ROWS, 7, stride=ROWS), :],
            jnp.zeros((1, 128), F32),
        ],
        axis=0,
    )


def load_keys(pieces, keys_v, rows_v, rows_s, sem):
    for k, piece in enumerate(pieces):
        key = piece[SB * ROWS : (SB + 1) * ROWS, :].astype(jnp.int32)
        keys_v[k * ROWS : (k + 1) * ROWS, :] = key & 7
        rows_v[k * ROWS : (k + 1) * ROWS, :] = key >> 3
    copy = pltpu.make_async_copy(rows_v, rows_s, sem)
    copy.start()
    return copy


def key_scratch(count):
    return [
        pltpu.VMEM((count * ROWS, 128), jnp.int32),
        pltpu.VMEM((count * ROWS, 128), jnp.int32),
        pltpu.SMEM((count * ROWS, 128), jnp.int32),
        pltpu.SemaphoreType.DMA,
    ]


def clear(groups):
    def body(n, c):
        for g in groups:
            g[pl.ds(pl.multiple_of(n * 128, 128), 128), :] = jnp.zeros((128, 128), F32)
        return c

    lax.fori_loop(0, 48, body, 0)


def scatter(lists, groups, stage, keys_v, rows_s, count):
    sub = lax.broadcasted_iota(jnp.int32, (LS, 128), 0)
    many = len(lists)

    def block(n, c):
        for a, (piece, row, at) in enumerate(lists):
            part = jnp.broadcast_to(keys_v[pl.ds(at + n, 1), :], (LS, 128))
            vals = jnp.where(sub == SB, 1.0, species_rows(piece, row + n))
            wide = jnp.concatenate([jnp.where(part == g, vals, 0.0) for g in range(8)], axis=0)
            stage[a][...] = wide.T
        for z in range(128):
            where = [rows_s[at + n, z] for _, _, at in lists]
            old = [groups[a][pl.ds(where[a], 1), :] for a in range(many)]
            new = [stage[a][z : z + 1, :] for a in range(many)]
            for a in range(many):
                groups[a][pl.ds(where[a], 1), :] = old[a] + new[a]
        return c

    lax.fori_loop(0, count, block, 0)


def own_sums_kernel(piece, out, *refs):
    g, stage = refs[:3], refs[3:7]
    keys_v, rows_v, rows_s, sem = refs[7:]
    copy = load_keys((piece,), keys_v, rows_v, rows_s, sem)
    groups = (out, *g)
    clear(groups)
    copy.wait()
    scatter([(piece, 8 * a, 8 * a) for a in range(4)], groups, stage, keys_v, rows_s, 8)

    def total(n, c):
        at = pl.ds(pl.multiple_of(n * 128, 128), 128)
        out[at, :] = (out[at, :] + g[0][at, :]) + (g[1][at, :] + g[2][at, :])
        return c

    lax.fori_loop(0, 48, total, 0)


def own_sums(piece):
    scratch = [pltpu.VMEM((6144, 128), F32)] * 3 + [pltpu.VMEM((128, 128), F32)] * 4 + key_scratch(1)
    return call(own_sums_kernel, "own_sums", [6144], [piece], scratch, us=10)[0]


def bin_sums_kernel(*refs):
    p = refs[0:3]
    g0, bins = refs[3:5]
    outs = refs[5:11]
    g = refs[11:17]
    stage = refs[17:23]
    keys_v, rows_v, rows_s, sem = refs[23:]
    copy = load_keys(p, keys_v, rows_v, rows_s, sem)
    clear(g)
    copy.wait()
    lists = [(p[a], h * 16, ROWS * a + h * 16) for a in range(3) for h in range(2)]
    scatter(lists, g, stage, keys_v, rows_s, 16)
    wide = stacked(bins[...])
    for blk in range(3):
        def project(n, c):
            total = []
            for r in (2 * n, 2 * n + 1):
                at = pl.ds(pl.multiple_of((blk * 16 + r) * 128, 128), 128)
                total.append(
                    ((g0[at, :] + g[0][at, :]) + (g[1][at, :] + g[2][at, :]))
                    + ((g[3][at, :] + g[4][at, :]) + g[5][at, :])
                )
            res = product(wide, jnp.concatenate(total, axis=1))
            for i in range(2):
                for h in range(2):
                    for k in range(4):
                        cut = k * 40 + h * 16
                        at = pl.ds(k * HALF + 2 * n + i, 18, stride=16)
                        outs[blk * 2 + h][at, :] = res[cut : cut + 18, i * 128 : (i + 1) * 128]
            return c

        lax.fori_loop(0, 8, project, 0, unroll=8)


def bin_sums(pieces, own, bins):
    scratch = [pltpu.VMEM((6144, 128), F32)] * 6 + [pltpu.VMEM((128, 128), F32)] * 6 + key_scratch(3)
    out = call(bin_sums_kernel, "bin_sums", [4 * HALF] * 6, [*pieces, own, bins], scratch, us=25)
    return out[0:2], out[2:4], out[4:6]


def gather(piece, out, proj, stage, keys_v, rows_s, at, base=0):
    first, second = stage[:2], stage[2:]

    def fetch(n, into):
        for a in range(2):
            for z in range(128):
                into[a][z : z + 1, :] = proj[pl.ds(rows_s[at + n * 2 + a, z], 1), :]

    def finish(n, held):
        for a in range(2):
            row = n * 2 + a
            part = jnp.broadcast_to(keys_v[pl.ds(at + row, 1), :], (LS, 128))
            wide = held[a][...].T
            mean = jnp.where(part == 0, wide[0:LS], 0.0)
            for g in range(1, 8):
                mean = jnp.where(part == g, wide[g * LS : (g + 1) * LS], mean)
            vals = species_rows(piece, row)
            res = vals + 0.5 * (mean - vals)
            out[pl.ds(base + row, 8, stride=ROWS), :] = res[0:8]
            out[pl.ds(base + row + 8 * ROWS, 6, stride=ROWS), :] = res[8:14]

    def block(n, c):
        fetch(2 * n + 1, second)
        finish(2 * n, first)
        fetch(jnp.minimum(2 * n + 2, ROWS // 2 - 1), first)
        finish(2 * n + 1, second)
        return c

    fetch(0, first)
    lax.fori_loop(0, ROWS // 4, block, 0)


def far_kernel(*refs):
    info, pieces = refs[0], refs[1:4]
    blocks = refs[4:10]
    table, outs, proj = refs[10], refs[11:14], refs[14]
    stage = refs[15:19]
    keys_v, rows_v, rows_s, sem = refs[19:]
    copy = load_keys(pieces, keys_v, rows_v, rows_s, sem)
    t = table[...]
    wide = stacked(t)
    weight = jnp.broadcast_to(jnp.sum(t, axis=1, keepdims=True), (128, 128))
    held = [((b + 4 - info[5]) & 3) * 256 for b in range(4)]
    for blk in range(3):
        def project(n, c):
            src = []
            for r in (2 * n, 2 * n + 1):
                rows = [
                    blocks[blk * 2 + h][pl.ds(held[b] + r, 16, stride=16), :]
                    for b in range(4) for h in range(2)
                ]
                src.append(jnp.concatenate(rows, axis=0))
            res = product(wide, jnp.concatenate(src, axis=1))
            for i in range(2):
                at = pl.ds(pl.multiple_of((blk * 16 + 2 * n + i) * 128, 128), 128)
                proj[at, :] = res[:, i * 128 : (i + 1) * 128] / weight
            return c

        lax.fori_loop(0, 8, project, 0, unroll=2)
    copy.wait()
    for a in range(3):
        gather(pieces[a], outs[a], proj, stage, keys_v, rows_s, a * ROWS)


def own_kernel(info, piece, proj, out, *refs):
    stage = refs[:4]
    keys_v, rows_v, rows_s, sem = refs[4:]
    load_keys((piece,), keys_v, rows_v, rows_s, sem).wait()
    gather(piece, out, proj, stage, keys_v, rows_s, 0, info[0] * ROWS)


def relax_far(info, pieces, blocks, table):
    scratch = [pltpu.VMEM((128, 128), F32)] * 4 + key_scratch(3)
    return call(
        far_kernel, "relax_far", [SB * ROWS] * 3 + [6144], [info, *pieces, *blocks, table], scratch, smem=1, us=20
    )


def relax_own(info, piece, proj):
    scratch = [pltpu.VMEM((128, 128), F32)] * 4 + key_scratch(1)
    return call(own_kernel, "relax_own", [S * ROWS], [info, piece, proj], scratch, smem=1, us=8)[0]


def swap_groups(tiles):
    lane = lax.broadcasted_iota(jnp.int32, (LS, 128), 1) // LS
    tiles = list(tiles)
    for d in (1, 2, 4):
        low = (lane & d) == 0
        for i in range(8):
            if i & d == 0:
                a, b = tiles[i], tiles[i + d]
                tiles[i] = jnp.where(low, a, pltpu.roll(b, LS * d, 1))
                tiles[i + d] = jnp.where(low, pltpu.roll(a, 128 - LS * d, 1), b)
    return tiles


def react_kernel(
    half, starts, info, q0, q1, q2, q3, moved, spread, rates, counts, matrix,
    out, h0, h1, h2, h3, numer,
):
    sums = (q0, q1, q2, q3)
    sends = (h0, h1, h2, h3)
    for k in range(4):
        for group in range(3):
            if group < 2:
                rows = sums[k][group * 128 : (group + 1) * 128, :]
            else:
                rows = jnp.concatenate([sums[k][256:HALF, :], jnp.zeros((96, 128), F32)], axis=0)
            turned = rows.T
            tiles = swap_groups([turned[g * LS : (g + 1) * LS] for g in range(8)])
            for b in range(8 if group < 2 else 2):
                numer[group * 8 + b, k * LS : (k + 1) * LS, :] = tiles[b]
    pad = jnp.zeros((2, 128), F32)

    def blend(n, k, rows):
        bottom = numer[n, SB : SB + 1, :] + 1.0
        tile = numer[n, k * LS : (k + 1) * LS, :]
        numer[n, k * LS : (k + 1) * LS, :] = (tile + jnp.concatenate([rows, pad], axis=0)) / bottom

    order = (1, 2, 3, 0)

    def own_bins(n, c):
        for k in order:
            at = starts[k] * 32 + n + (16 * half - 1)
            rows = jnp.concatenate(
                [moved[pl.ds(at, 8, stride=32), :], moved[pl.ds(at + 256, 6, stride=32), :]], axis=0
            )
            blend(n, k, rows)
        return c

    edge, ref, there = ((0, q1, info[5] > 0), (17, q3, info[5] < 3))[half]
    for k in order:
        blend(edge, k, jnp.where(there, ref[pl.ds(HALF + starts[k], SB), :], 0.0))
    lax.fori_loop(1 - half, 18 - half, own_bins, 0, unroll=True)
    m_hi, m_lo = split(matrix[...])
    wide_m = jnp.concatenate([m_hi, m_lo, m_hi], axis=1)
    many = 8

    def bins(group, c):
        cells, scale = [], []
        for i in range(many):
            n = group * many + i
            b = 16 * half + n
            mid = numer[n + 1]
            cells.append(mid + spread[pl.ds(b, 1), :] * (numer[n + 2] - 2.0 * mid + numer[n]))
            scale.append(0.5 * rates[pl.ds(b, 1), :])
        state_now = jnp.concatenate(cells, axis=1)
        scale = jnp.concatenate(scale, axis=1)
        left = jnp.concatenate([counts[...]] * many, axis=1)
        for substep in range(4):
            hi, lo = split(state_now)
            rate = jnp.dot(
                wide_m, jnp.concatenate([hi, hi, lo], axis=0), preferred_element_type=F32
            )
            step = jnp.where(substep < left, scale, 0.0)
            state_now = state_now + step * jnp.tanh(rate)
        for k in range(4):
            tiles = swap_groups(
                [state_now[k * LS : (k + 1) * LS, i * 128 : (i + 1) * 128] for i in range(8)]
            )
            at = pl.ds(pl.multiple_of(group * 128, 128), 128)
            sends[k][at, :] = jnp.concatenate(tiles, axis=0).T
        for i in range(many):
            n = group * many + i
            cell = state_now[:, i * 128 : (i + 1) * 128]
            for k in range(4):
                at = starts[k] * 16 + n
                out[pl.ds(at, 8, stride=16), :] = cell[k * LS : k * LS + 8]
                out[pl.ds(at + 128, 6, stride=16), :] = cell[k * LS + 8 : k * LS + SB]
        return c

    lax.fori_loop(0, 16 // many, bins, 0, unroll=True)


def react(half, starts, info, sums, moved, spread, rates, counts, matrix):
    return call(
        functools.partial(react_kernel, half), "react_upper" if half else "react_lower",
        [S * 16] + [256] * 4,
        [starts, info, *sums, moved, spread, rates, counts, matrix],
        [pltpu.VMEM((18, 64, 128), F32)], smem=2, us=6,
    )


def shift(array, axis, by):
    count = lax.axis_size(axis)
    return lax.ppermute(array, axis, [(n, (n + by) % count) for n in range(count)])


def on_device(
    les_state, cmc_state, cmc_map, pdf_index, pdf_table, diffusion, chem_matrix,
    dissipation, reaction_rate, substeps,
):
    highest = lax.Precision.HIGHEST
    i, j = lax.axis_index("slab"), lax.axis_index("cross")
    peer = [lax.rem(j + k, 4) for k in range(4)]
    source = [lax.rem(j + 4 - k, 4) for k in range(4)]

    def start(block):
        return jnp.minimum(block * SB, S - SB)

    info = jnp.stack([start(p) for p in peer] + [i, j, jnp.int32(lax.axis_size("slab"))]).astype(jnp.int32)
    starts = jnp.stack([start(p) for p in source]).astype(jnp.int32)
    les = les_state.reshape(S * ROWS, 128)
    cmc = cmc_state.reshape(S * 32, 128)
    up, down, y_up, y_down = call(edges_kernel, "edges", [EDGE + 16] * 2 + [S * 8] * 2, [les, cmc])
    low, high = shift(up, "slab", 1), shift(down, "slab", -1)
    y_low, y_high = shift(y_up, "cross", 1), shift(y_down, "cross", -1)
    turned = jnp.pad(pdf_table.T, ((1, 7), (0, 0)))
    bins = jnp.concatenate([lax.dynamic_slice_in_dim(turned, p * 32, 40, 0) for p in peer], 0)
    lane = jnp.arange(64, dtype=jnp.int32)
    held = start(lax.rem(j + 4 - lane // LS, 4))
    pick = ((held + lane % LS)[:, None] == jnp.arange(S)[None, :]) & (lane % LS < SB)[:, None]
    again = (held == S - SB) & (lane % LS < 4 * SB - S)
    once = pick & ~again[:, None]
    matrix = jnp.dot(pick.astype(F32), chem_matrix, precision=highest)
    matrix = jnp.einsum("ab,cb->ac", matrix, once.astype(F32), precision=highest)
    y_low, bins, matrix, starts = lax.optimization_barrier((y_low, bins, matrix, starts))
    pieces = call(
        transport_kernel, "transport", [(SB + 1) * ROWS] * 4,
        [info, diffusion, les, low, high, y_low, y_high, cmc_map.reshape(ROWS, 128), pdf_index.reshape(ROWS, 128)],
        [pltpu.VMEM((S * ROWS, 128), F32)] * 2, smem=2,
    )
    pieces = [pieces[0]] + [shift(pieces[k], "cross", k) for k in (1, 2, 3)]
    own = own_sums(pieces[0])
    below, here, above = bin_sums(pieces[1:], own, bins)
    got = [(shift(below[h], "slab", -1), shift(above[h], "slab", 1)) for h in range(2)]
    cmc, here = lax.optimization_barrier((cmc, here))
    moved, b_up, b_down = call(advect_kernel, "advect", [S * 32, S, S], [info, cmc, low, high], smem=1)
    here, moved = lax.optimization_barrier((here, moved))
    cat = jnp.concatenate
    sums = []
    for h in range(2):
        total = here[h] + got[h][0] + got[h][1]
        part = [total[k * HALF : (k + 1) * HALF] for k in range(4)]
        if h:
            part[3] = cat([part[3], b_down], 0)
        else:
            part[1] = cat([part[1], b_up], 0)
        sums.append([part[0]] + [shift(part[k], "cross", k) for k in (1, 2, 3)])
    halves, sends = [], []
    for h in range(2):
        if h:
            sums[1], halves[0] = lax.optimization_barrier((sums[1], halves[0]))
        state, *parts = react(
            h, starts, info, sums[h], moved, dissipation, reaction_rate, substeps.reshape(1, 128), matrix
        )
        halves.append(state)
        sends.append(parts)
    low, high, here = [], [], []
    for h in range(2):
        if h:
            sends[1], got = lax.optimization_barrier((sends[1], got))
        got = [sends[h][0]] + [shift(sends[h][k], "cross", -k) for k in (1, 2, 3)]
        here.append(got)
    for h in range(2):
        here[h] = cat(lax.optimization_barrier(here[h]), 0)
        low.append(shift(here[h], "slab", 1))
        high.append(shift(here[h], "slab", -1))
    cmc_out = cat([half.reshape(S, 16, 128) for half in halves], 1)
    *done, proj = relax_far(info, pieces[1:], [*low, *here, *high], pdf_table)
    parts = [relax_own(info, pieces[0], proj)] + [shift(done[k - 1], "cross", -k) for k in (1, 2, 3)]
    parts = lax.optimization_barrier(parts)
    les_out = parts[0]
    for k in (1, 2, 3):
        les_out = lax.dynamic_update_slice_in_dim(les_out, parts[k], start(peer[k]) * ROWS, 0)
    return les_out.reshape(les_state.shape), cmc_out


def solution(mesh):
    return jax.shard_map(
        on_device,
        mesh=mesh,
        in_specs=(
            P(None, "slab", "cross", None),
            P(None, "cross", "slab"),
            P("slab", "cross", None),
            P("slab", "cross", None),
            P(),
            P(),
            P(),
            P("cross", "slab"),
            P("cross", "slab"),
            P("slab"),
        ),
        out_specs=(P(None, "slab", "cross", None), P(None, "cross", "slab")),
        check_vma=False,
    )
```
